256 devices in a mesh: section: 4 (over z_hi), vit: 16 (over y, x), dp: 4 (over z_lo, core).
Axes of the slice: x: 4, y: 4, z: 8 (z_hi: 4, z_lo: 2; z = z_hi * 2 + z_lo), core: 2. Of those that a mesh axis runs over, the one named last changes fastest.
Arguments:
- grad_llm: bfloat16 [4, 8192, 4096], P('section', ('dp', 'vit')), parts along dimension 1, may hold values from -6 to 6
- vis_slot: int32 [64, 128], P('dp'), parts along dimension 0, may hold values from 0 to 2047, as said below
- image_rows: int32 [16, 16], P('dp'), parts along dimension 0, may hold values from 8 to 32, as said below
- section_layer: int32 [4], replicated, may hold values from 0 to 3, each once
- vit_in: bfloat16 [32768, 1152], P(('dp', 'section', 'vit')), parts along dimension 0, may hold values from -6 to 6
- vit_out: bfloat16 [32768, 1152], P(('dp', 'section', 'vit')), parts along dimension 0, may hold values from -6 to 6
- ln_gain: float32 [1152], replicated, may hold values from 0.5 to 1.5
- ln_bias: float32 [1152], replicated, may hold values from -3 to 3
- qkv_weight: bfloat16 [1152, 3456], P('section'), may hold values from -0.1875 to 0.1875
- proj_weight: bfloat16 [1152, 1152], P('section'), may hold values from -0.1875 to 0.1875
- merge_gain: float32 [1152], replicated, may hold values from 0.5 to 1.5
- merge_bias: float32 [1152], replicated, may hold values from -3 to 3
- fc1_weight: bfloat16 [4608, 4608], P(None, 'vit'), may hold values from -0.09375 to 0.09375
- fc1_bias: float32 [4608], P('vit'), may hold values from -3 to 3
- fc2_weight: bfloat16 [4608, 4096], P('vit'), may hold values from -0.09375 to 0.09375
Outputs:
- vit_grad: bfloat16 [32768, 1152], P(('dp', 'section', 'vit')), parts along dimension 0
The draws below stay inside these ranges and needn't reach their ends.
There are 4 independent parts, one for each index of `dp`. The reference program is written for one: setup_inputs(seed, part) draws one part's arguments, and reference() takes and returns one part's arrays. A program takes and returns all parts, laid end to end along the dimension named above; an argument that names none is the same for every part. Nothing has to cross between parts.
Inputs may be any that keep to these rules, and one draw needn't show every extreme that they name: `vis_slot`: every slot number appears once. On every language-model device v, the rows d * 2 to d * 2 + 1 name 2 consecutive slots that start at a multiple of 2 inside d * 32 to d * 32 + 31, the slots of vision device d (devices numbered with the group first). `image_rows`: in every group one image has exactly 32 merged tokens. `section_layer`: A permutation; the section with value 3 holds no DeepStack layer.
All inputs are finite; a program needn't handle non-finite values.
Results may differ from the reference program's by a relative error of at most 0.02.
Values may be sent and summed in bfloat16 or wider, within the bound.
A program may use at most 128 MiB of HBM per device.

```python
import jax
import jax.numpy as jnp
from jax import lax

DV = 1152
HEADS = 16
DL = 4096
LEVELS = 3
SLOTS = 32
HD = 72
DM = 4608
RUN = 2
LLM_ROWS = 128
IMAGES = 16
GROUP_SLOTS = 512
N_SECTION = 4
N_VIT = 16


def draw_vis_slot(key, part):
    devices = N_SECTION * N_VIT
    device_keys = jax.random.split(jax.random.fold_in(key, 11), devices)
    orders = jax.vmap(jax.random.permutation, in_axes=(0, None))(device_keys, N_VIT).astype(jnp.int32)
    device_id = jnp.arange(devices, dtype=jnp.int32)
    within = jnp.arange(RUN, dtype=jnp.int32)
    slots = device_id[None, :, None] * SLOTS + RUN * orders.T[:, :, None] + within[None, None, :]
    return slots.reshape(N_VIT, LLM_ROWS).astype(jnp.int32)


def draw_image_rows(key, part):
    counts = jax.random.randint(jax.random.fold_in(key, 3), (N_SECTION, IMAGES), SLOTS // 4, SLOTS + 1)
    chosen = jax.random.randint(jax.random.fold_in(key, 5), (N_SECTION, 1), 0, IMAGES)
    column = jnp.arange(IMAGES, dtype=jnp.int32)[None, :]
    return jnp.where(column == chosen, SLOTS, counts).astype(jnp.int32)


def levels(rng, dims, shards, smallest, top_value):
    level, own = 1.0, jax.random.fold_in(rng, 6)
    for dim, parts in shards:
        draws = jnp.exp(jax.random.uniform(jax.random.fold_in(own, dim), (parts,), jnp.float32, smallest / len(shards), top_value / len(shards)))
        level = level * jnp.repeat(draws, dims[dim] // parts).reshape([-1 if axis == dim else 1 for axis in range(len(dims))])
    return level


def centred(rng, extent, deviation, reach, pieces=(), kind=jnp.bfloat16):
    level = levels(rng, extent, pieces, -0.22, 0.18) if pieces else 1.0
    values = jax.random.normal(rng, extent, jnp.float32) * deviation * level
    return jnp.minimum(jnp.maximum(values, -reach), reach).astype(kind)


def setup_inputs(seed: int = 0, part: int = 0) -> dict:
    streams_of = jax.random.split(jax.random.key(seed), 16)
    own_keys = jax.random.split(jax.random.fold_in(streams_of[15], part), 16)
    return {
        "grad_llm": centred(own_keys[0], (N_SECTION, N_VIT * LLM_ROWS, DL), 1.0, 6.0, ((0, 4), (1, 16))),
        "vis_slot": draw_vis_slot(jax.random.fold_in(jax.random.fold_in(streams_of[15], part), 71), part),
        "image_rows": draw_image_rows(jax.random.fold_in(jax.random.fold_in(streams_of[15], part), 71), part),
        "section_layer": jax.random.permutation(streams_of[3], N_SECTION).astype(jnp.int32),
        "vit_in": centred(own_keys[4], (N_SECTION * GROUP_SLOTS * 4, DV), 1.0, 6.0, ((0, 64),)),
        "vit_out": centred(own_keys[5], (N_SECTION * GROUP_SLOTS * 4, DV), 1.0, 6.0, ((0, 64),)),
        "ln_gain": jnp.clip(1.0 + 0.1 * jax.random.normal(streams_of[6], (DV,), jnp.float32), 0.5, 1.5),
        "ln_bias": centred(streams_of[7], (DV,), 0.5, 3.0, (), jnp.float32),
        "qkv_weight": centred(streams_of[8], (DV, 3 * DV), DV ** -0.5, 0.1875, ((0, 4),)),
        "proj_weight": centred(streams_of[9], (DV, DV), DV ** -0.5, 0.1875, ((0, 4),)),
        "merge_gain": jnp.clip(1.0 + 0.1 * jax.random.normal(streams_of[10], (DV,), jnp.float32), 0.5, 1.5),
        "merge_bias": centred(streams_of[11], (DV,), 0.5, 3.0, (), jnp.float32),
        "fc1_weight": centred(streams_of[12], (DM, DM), DM ** -0.5, 0.09375, ((1, 16),)),
        "fc1_bias": centred(streams_of[13], (DM,), 0.5, 3.0, ((0, 16),), jnp.float32),
        "fc2_weight": centred(streams_of[14], (DM, DL), DM ** -0.5, 0.09375, ((0, 16),)),
    }


norm_eps = 1e-06

def normalize(values):
    row_mean = lax.optimization_barrier(jnp.mean(values, axis=-1, keepdims=True))
    centered = values - row_mean
    variance = lax.optimization_barrier(jnp.mean(centered * centered, axis=-1, keepdims=True))
    inverse = lax.rsqrt(variance + norm_eps)
    return (centered * inverse, inverse)

def normalize_back(upstream, normed_rows, inverse, gain):
    scaled = upstream * gain
    mean_scaled = lax.optimization_barrier(jnp.mean(scaled, axis=-1, keepdims=True))
    mean_cross = lax.optimization_barrier(jnp.mean(scaled * normed_rows, axis=-1, keepdims=True))
    return (scaled - mean_scaled - normed_rows * mean_cross) * inverse

def gelu_slope(pre_act):
    cumulative = 0.5 * (1.0 + lax.erf(pre_act * 0.7071067811865476))
    density = jnp.exp(-0.5 * pre_act * pre_act) * 0.3989422804014327
    return cumulative + pre_act * density

def slot_layout(image_rows):
    image_ends = jnp.cumsum(image_rows, axis=1).astype(jnp.int32)
    position = jnp.arange(GROUP_SLOTS, dtype=jnp.int32)
    slot_image = lax.optimization_barrier(jnp.sum((position[None, :, None] >= image_ends[:, None, :]).astype(jnp.int32), axis=2))
    slot_live = position[None, :] < image_ends[:, -1:]
    return (slot_image, slot_live)

def reference(grad_llm, vis_slot, image_rows, section_layer, vit_in, vit_out, ln_gain, ln_bias, qkv_weight, proj_weight, merge_gain, merge_bias, fc1_weight, fc1_bias, fc2_weight):
    all_slots = N_SECTION * GROUP_SLOTS
    section_weight = jnp.where(section_layer < LEVELS, (section_layer + 1).astype(jnp.float32) / LEVELS, 0.0).astype(jnp.float32)
    summed = jnp.zeros((N_VIT * LLM_ROWS, DL), jnp.float32)
    for section_index in range(N_SECTION):
        summed = summed + section_weight[section_index] * grad_llm[section_index].astype(jnp.float32)
    placed = jnp.zeros((all_slots, DL), jnp.float32).at[vis_slot.reshape(-1)].set(summed)
    slot_image, slot_live = slot_layout(image_rows)
    merged_grad = jnp.where(slot_live.reshape(-1)[:, None], placed, 0.0).astype(jnp.bfloat16)
    out_rows, out_inverse = normalize(vit_out.astype(jnp.float32))
    merge_in = (out_rows * merge_gain + merge_bias).astype(jnp.bfloat16).reshape(all_slots, DM)
    pre_act = jnp.dot(merge_in, fc1_weight, preferred_element_type=jnp.float32) + fc1_bias
    hidden_grad = jnp.dot(merged_grad, fc2_weight.T, preferred_element_type=jnp.float32)
    pre_grad = (hidden_grad * gelu_slope(pre_act)).astype(jnp.bfloat16)
    block_width = DM // N_VIT
    merge_grad = jnp.zeros((all_slots, DM), jnp.float32)
    for block_index in range(N_VIT):
        first = block_index * block_width
        block_term = jnp.dot(pre_grad[:, first:first + block_width], fc1_weight[:, first:first + block_width].T, preferred_element_type=jnp.float32)
        rounded = lax.optimization_barrier(block_term.astype(jnp.bfloat16))
        merge_grad = merge_grad + rounded.astype(jnp.float32)
    out_grad = normalize_back(merge_grad.reshape(-1, DV), out_rows, out_inverse, merge_gain).astype(jnp.bfloat16)
    in_rows, in_inverse = normalize(vit_in.astype(jnp.float32))
    normed = (in_rows * ln_gain + ln_bias).astype(jnp.bfloat16)
    projected = jnp.dot(normed, qkv_weight, preferred_element_type=jnp.float32).astype(jnp.bfloat16)
    out_proj_grad = jnp.dot(out_grad, proj_weight.T, preferred_element_type=jnp.float32).astype(jnp.bfloat16)
    length = 4 * GROUP_SLOTS
    per_head = projected.reshape(N_SECTION, length, 3, HEADS, HD).transpose(2, 0, 3, 1, 4).reshape(3, N_SECTION * HEADS, length, HD)
    grad_heads = out_proj_grad.reshape(N_SECTION, length, HEADS, HD).transpose(0, 2, 1, 3).reshape(N_SECTION * HEADS, length, HD)
    patch_image = jnp.repeat(slot_image, 4, axis=1)
    patch_live = jnp.repeat(slot_live, 4, axis=1)
    group_of = (jnp.arange(N_SECTION * HEADS, dtype=jnp.int32) // HEADS).astype(jnp.int32)
    score_scale = HD ** (-0.5)

    def one_head(inputs):
        query_rows, key_rows, value_rows, grad_rows, group_index = inputs
        image_here = lax.dynamic_index_in_dim(patch_image, group_index, 0, keepdims=False)
        live_here = lax.dynamic_index_in_dim(patch_live, group_index, 0, keepdims=False)
        scores = jnp.dot(query_rows, key_rows.T, preferred_element_type=jnp.float32) * score_scale
        allowed = (image_here[:, None] == image_here[None, :]) & live_here[:, None] & live_here[None, :]
        exponent = jnp.where(allowed, jnp.exp(jnp.where(allowed, scores, 0.0)), 0.0)
        denominator = lax.optimization_barrier(jnp.sum(exponent, axis=1, keepdims=True)) + 1.0 - live_here.astype(jnp.float32)[:, None]
        softmax_weights = (exponent / denominator).astype(jnp.bfloat16)
        prob_grad = jnp.dot(grad_rows, value_rows.T, preferred_element_type=jnp.float32)
        weighted = softmax_weights.astype(jnp.float32)
        row_dot = lax.optimization_barrier(jnp.sum(weighted * prob_grad, axis=1, keepdims=True))
        score_grad = (weighted * (prob_grad - row_dot) * score_scale).astype(jnp.bfloat16)
        query_grad = jnp.dot(score_grad, key_rows, preferred_element_type=jnp.float32).astype(jnp.bfloat16)
        key_grad = jnp.dot(score_grad.T, query_rows, preferred_element_type=jnp.float32).astype(jnp.bfloat16)
        value_grad = jnp.dot(softmax_weights.T, grad_rows, preferred_element_type=jnp.float32).astype(jnp.bfloat16)
        return jnp.stack([query_grad, key_grad, value_grad])
    head_grads = lax.map(one_head, (per_head[0], per_head[1], per_head[2], grad_heads, group_of))
    projected_grad = head_grads.reshape(N_SECTION, HEADS, 3, length, HD).transpose(0, 3, 2, 1, 4).reshape(all_slots * 4, 3 * DV)
    normed_grad = jnp.dot(projected_grad, qkv_weight.T, preferred_element_type=jnp.float32)
    vit_grad = (out_grad.astype(jnp.float32) + normalize_back(normed_grad, in_rows, in_inverse, ln_gain)).astype(jnp.bfloat16)
    return vit_grad
```

```python
import functools

import jax
import jax.numpy as jnp
from jax import lax
from jax.experimental import pallas as pl
from jax.experimental.pallas import tpu as pltpu
from jax.sharding import PartitionSpec as P

HEADS = 16
LEVELS = 3
DV = 1152
DM = 4608
DL = 4096
HD = 72
SLOTS = 32
PATCHES = 128
WINDOW = 384
HIDDEN = 288
HALF = DM // 2
SCALE = HD**-0.5
norm_eps = 1e-06
MESH = pl.DeviceIdType.MESH
F32 = jnp.float32
BF16 = jnp.bfloat16

NN = (((1,), (0,)), ((), ()))
NT = (((1,), (1,)), ((), ()))


def dot(a, b, dims=NN):
    return lax.dot_general(a, b, dims, preferred_element_type=F32)


def normalize(values):
    row_mean = jnp.mean(values, axis=-1, keepdims=True)
    centered = values - row_mean
    variance = jnp.mean(centered * centered, axis=-1, keepdims=True)
    inverse = lax.rsqrt(variance + norm_eps)
    return (centered * inverse, inverse)


def normalize_back(upstream, normed_rows, inverse, gain):
    scaled = upstream * gain
    mean_scaled = jnp.mean(scaled, axis=-1, keepdims=True)
    mean_cross = jnp.mean(scaled * normed_rows, axis=-1, keepdims=True)
    return (scaled - mean_scaled - normed_rows * mean_cross) * inverse


def gelu_slope(pre_act):
    cumulative = 0.5 * (1.0 + lax.erf(pre_act * 0.7071067811865476))
    density = jnp.exp(-0.5 * pre_act * pre_act) * 0.3989422804014327
    return cumulative + pre_act * density


class Place:
    def __init__(self):
        self.s = lax.axis_index("section")
        v = lax.axis_index("vit")
        d = lax.axis_index("dp")
        self.x, self.y = lax.rem(v, 4), v // 4
        self.c, self.zl = lax.rem(d, 2), d // 2
        self.z = self.s * 2 + self.zl
        self.v = v

    def at(self, dx=0, dy=0):
        x, y = lax.rem(self.x + dx + 4, 4), lax.rem(self.y + dy + 4, 4)
        return {"section": self.s, "vit": y * 4 + x, "dp": self.zl * 2 + self.c}

    def up(self, dz):
        z = lax.rem(self.z + dz + 8, 8)
        return {"section": z // 2, "vit": self.v, "dp": lax.rem(z, 2) * 2 + self.c}

    def other_core(self):
        return {"section": self.s, "vit": self.v, "dp": self.zl * 2 + 1 - self.c}

    def along(self, dv):
        return {"section": self.s, "vit": lax.rem(self.v + dv + 16, 16), "dp": self.zl * 2 + self.c}


class Copies:
    def __init__(self, ssem, rsem):
        self.ssem, self.rsem, self.made = ssem, rsem, []

    def make(self, src, dst, device):
        k = len(self.made)
        copy = pltpu.make_async_remote_copy(
            src, dst, self.ssem.at[k], self.rsem.at[k], device_id=device, device_id_type=MESH
        )
        self.made.append(copy)
        return copy

    def drain(self):
        for copy in self.made:
            copy.wait_send()


class PlaneGather:
    def __init__(self, place, copies, buf, width, split):
        self.parts = []
        for axis in (0, 1):
            cols = pl.ds(0, split) if axis == 0 else pl.ds(split, width - split)

            def block(d1, d2, axis=axis):
                dx, dy = (d1, d2) if axis == 0 else (d2, d1)
                return lax.rem(place.y + dy + 4, 4) * 4 + lax.rem(place.x + dx + 4, 4)

            def first(d, axis=axis):
                return place.at(d, 0) if axis == 0 else place.at(0, d)

            def second(d, axis=axis):
                return place.at(0, d) if axis == 0 else place.at(d, 0)

            def send(d1, d2, rows, device, block=block, cols=cols):
                ref = buf.at[block(d1, d2), rows, cols]
                return copies.make(ref, ref, device)

            every, low, high = pl.ds(0, 32), pl.ds(0, 16), pl.ds(16, 16)
            part = {
                "s1p": send(0, 0, every, first(1)),
                "s1m": send(0, 0, every, first(-1)),
                "f1p": send(-1, 0, low, first(1)),
                "f1m": send(1, 0, high, first(-1)),
            }
            for d1 in (0, -1, 1, 2):
                part["s2p", d1] = send(d1, 0, every, second(1))
                part["s2m", d1] = send(d1, 0, every, second(-1))
                part["f2p", d1] = send(d1, -1, low, second(1))
                part["f2m", d1] = send(d1, 1, high, second(-1))
            self.parts.append(part)

    def start(self):
        for p in self.parts:
            for k in ("s1p", "s1m", ("s2p", 0), ("s2m", 0)):
                p[k].start()

    def near(self):
        for p in self.parts:
            p["s1p"].wait_recv()
            p["f1p"].start()
            p["s2p", -1].start()
            p["s2m", -1].start()
            p["s1m"].wait_recv()
            p["f1m"].start()
            p["s2p", 1].start()
            p["s2m", 1].start()

    def far(self):
        for p in self.parts:
            p["f1p"].wait_recv()
            p["f1m"].wait_recv()
            p["s2p", 2].start()
            p["s2m", 2].start()

    def pass_on(self, d1):
        for p in self.parts:
            p["s2p", d1].wait_recv()
            p["f2p", d1].start()
            p["s2m", d1].wait_recv()
            p["f2m", d1].start()

    def finish(self):
        for d1 in (0, -1, 1, 2):
            for p in self.parts:
                p["f2p", d1].wait_recv()
                p["f2m", d1].wait_recv()


class WeightGather:
    def __init__(self, place, copies, qkv, proj):
        s, c, zl = place.s, place.c, place.zl
        self.odd = zl == 1
        self.even = zl == 0
        chunks = [
            (qkv, 48, n * 48, 3456, 1792) for n in range(3)
        ] + [(proj, 144, 0, 1152, 640)]

        def piece(chunk, section, side):
            ref, rows, offset, width, split = chunk
            start = pl.multiple_of(lax.rem(section + 8, 4) * 288 + c * 144 + offset, 16)
            cols = {
                0: pl.ds(0, width), 1: pl.ds(0, split), 2: pl.ds(split, width - split)
            }[side]
            return ref.at[pl.ds(start, rows), cols]

        def make(chunk, section, side, device):
            ref = piece(chunk, section, side)
            return copies.make(ref, ref, device)

        right, left, core = place.up(1), place.up(-1), place.other_core()
        self.right, self.left = [], []
        for ch in chunks:
            self.right.append((
                make(ch, s - 1 + zl, 0, right),
                make(ch, s - 1, 0, core),
                make(ch, s - 2 + zl, 1, right),
                make(ch, s - 2, 1, core),
            ))
            self.left.append((
                make(ch, s + zl, 0, left),
                make(ch, s + 1, 0, core),
                make(ch, s + zl + 1, 2, left),
                make(ch, s + 2, 2, core),
            ))

    def start(self):
        @pl.when(self.odd)
        def _():
            for whole, *_ in self.right:
                whole.start()

        @pl.when(self.even)
        def _():
            for whole, *_ in self.left:
                whole.start()

    def whole(self, n):
        for lead, follow, side in ((self.odd, self.even, self.right), (self.even, self.odd, self.left)):
            whole, core, part, _ = side[n]
            whole.wait_recv()
            core.start()
            pl.when(follow)(whole.start)
            pl.when(lead)(part.start)

    def part(self, n):
        for follow, side in ((self.even, self.right), (self.odd, self.left)):
            _, _, part, core = side[n]
            part.wait_recv()
            core.start()
            pl.when(follow)(part.start)

    def finish(self):
        for side in (self.right, self.left):
            for _, core, _, core_part in side:
                core.wait_recv()
                core_part.wait_recv()


def body(
    grad, vit_in, vit_out, qkv_w, proj_w, fc1_w, fc2_w,
    section_weight, slot_pos, live_slot, id_row, id_col, live_row,
    ln_gain, ln_bias, merge_gain, merge_bias, fc1_bias,
    out_ref,
    xo, xin, rows_in, rows_grad, zin, zown, fc1, fc2, qkv, proj,
    h_out, r_out, h_in, r_in, wide, slope, hidden, pre_grad,
    ps, rb1, rb2, qs, rb3, merge_total, og,
    t32, heads, k_rows, v_rows, probs, o_cols, pg, strips, ssem, rsem, lsem,
):
    place = Place()
    s, x, y = place.s, place.x, place.y
    copies = Copies(ssem, rsem)

    near = [place.at(1, 0), place.at(-1, 0), place.at(2, 0), place.at(0, 1), place.at(0, -1), place.at(0, 2)]
    near += [place.up(1), place.up(-1), place.up(2), place.up(-2), place.up(4), place.other_core()]
    near += [place.along(1), place.along(-1)]
    barrier = pltpu.get_barrier_semaphore()
    for device in near:
        pl.semaphore_signal(barrier, inc=1, device_id=device, device_id_type=MESH)

    own_rows = pl.ds(pl.multiple_of(s * 288, 16), 288)
    group_rows = pl.ds(pl.multiple_of(s * 32, 32), 32)
    local = [
        pltpu.make_async_copy(src, dst, lsem.at[k])
        for k, (src, dst) in enumerate((
            (vit_out, xo),
            (grad.at[group_rows], zown),
            (vit_in, xin.at[1]),
            (fc1_w, fc1),
            (qkv_w, qkv.at[own_rows]),
            (proj_w, proj.at[own_rows]),
            (fc2_w, fc2),
        ))
    ]
    for copy in local:
        copy.start()

    me = place.v
    local[0].wait()
    h, r = normalize(xo[...].astype(F32))
    h_out[...] = h
    r_out[...] = r
    value = h * merge_gain[...] + merge_bias[...]
    for t in range(9):
        strips[t] = value[:, 128 * t : 128 * t + 128]
    for p in range(4):
        for t in range(9):
            strip = strips[t, pl.ds(p, SLOTS, stride=4), :]
            rows_in[me, :, pl.ds(DV * p + 128 * t, 128)] = strip.astype(BF16)

    pl.semaphore_wait(barrier, len(near))

    z_copies = []
    for d in (1, 2, 3):
        rows = pl.ds(pl.multiple_of(lax.rem(s + d, 4) * 32, 32), 32)
        z_copies.append(copies.make(grad.at[rows], zin.at[d - 1], place.up(2 * d)))
    for copy in (z_copies[0], z_copies[2], z_copies[1]):
        copy.start()
    gather_in = PlaneGather(place, copies, rows_in, DM, HALF)
    gather_in.start()
    halo_in = [
        copies.make(vit_in, xin.at[0], place.along(1)),
        copies.make(vit_in, xin.at[2], place.along(-1)),
    ]
    for copy in halo_in:
        copy.start()
    gather_grad = PlaneGather(place, copies, rows_grad, DL, DL // 2)
    weights = WeightGather(place, copies, qkv, proj)

    gather_in.near()
    gather_in.pass_on(0)
    gather_in.far()

    for copy in z_copies:
        copy.wait_recv()
    for copy in (local[1], local[4], local[5]):
        copy.wait()
    weights.start()

    @pl.loop(0, 4)
    def _(i):
        cols = pl.ds(pl.multiple_of(i * 1024, 128), 1024)
        total = section_weight[0, s] * zown[:, cols].astype(F32)
        for d in (1, 2, 3):
            total += section_weight[0, lax.rem(s - d + 4, 4)] * zin[d - 1, :, cols].astype(F32)
        rows_grad[me, :, cols] = total.astype(BF16)

    gather_grad.start()
    gather_in.pass_on(-1)
    gather_in.pass_on(1)
    gather_in.pass_on(2)
    weights.whole(0)
    gather_grad.near()
    gather_in.finish()
    local[3].wait()

    def fill_slope(lo, hi):
        @pl.loop(lo, hi)
        def _(i):
            block = rows_in[pl.ds(i * 4, 4)].reshape(128, DM)
            rows = pl.ds(pl.multiple_of(i * 128, 128), 128)
            slope[rows, :] = gelu_slope(dot(block, fc1[...], NT) + fc1_bias[...])

    fill_slope(0, 2)
    gather_grad.pass_on(0)
    gather_grad.far()
    fill_slope(2, 4)
    weights.whole(1)
    gather_grad.pass_on(-1)
    gather_grad.pass_on(1)
    weights.whole(2)
    gather_grad.pass_on(2)
    local[6].wait()
    gather_grad.finish()

    @pl.loop(0, 4)
    def _(i):
        block = rows_grad[pl.ds(i * 4, 4)].reshape(128, DL)
        rows = pl.ds(pl.multiple_of(i * 128, 128), 128)
        hidden[rows, :] = dot(block, fc2[...], NT)

    value = hidden[...]
    high = value.astype(BF16)
    low = (value - high.astype(F32)).astype(BF16)
    for i in range(4):
        slots = lax.broadcasted_iota(jnp.int32, (128, 512), 0) + 128 * i
        chosen = jnp.where(slots == slot_pos[...], 1.0, 0.0).astype(BF16)
        placed = dot(chosen, high) + dot(chosen, low)
        rows = pl.ds(128 * i, 128)
        live = live_slot[rows, :] > 0.0
        block = jnp.where(live, placed, 0.0) * slope[rows, :]
        pre_grad[pl.ds(4 * i, 4)] = block.astype(BF16).reshape(4, SLOTS, HIDDEN)

    def token(part, d1, d2):
        dx, dy = (d1, d2) if part == 0 else (d2, d1)
        return lax.rem(y + dy, 4) * 4 + lax.rem(x + dx, 4)

    def first(part, d):
        return place.at(d, 0) if part == 0 else place.at(0, d)

    def second(part, d):
        return place.at(0, d) if part == 0 else place.at(d, 0)

    def product(part, d1):
        block = jnp.concatenate([pre_grad[token(part, d1, d2)] for d2 in range(4)], axis=0)

        @pl.loop(0, 6)
        def _(i):
            start = pl.multiple_of(i * 384, 128)
            cols = pl.ds(pl.multiple_of(start + part * HALF, 128), 384)
            term = dot(block, fc1[:, cols]).astype(BF16).reshape(4, SLOTS, 384)
            ps[part, d1, :, :, pl.ds(start, 384)] = term

    def scatter(part):
        low, high = pl.ds(0, 2), pl.ds(2, 2)
        near1, near2 = first(part, 1), first(part, -1)
        return {
            "1p": copies.make(ps.at[part, 2, low], rb1.at[part, 0], near1),
            "1m": copies.make(ps.at[part, 2, high], rb1.at[part, 1], near2),
            "2p": [copies.make(ps.at[part, 1, k], rb2.at[part, 0, k], near1) for k in range(4)],
            "2m": [copies.make(ps.at[part, 3, k], rb2.at[part, 1, k], near2) for k in range(4)],
            "3": [copies.make(qs.at[part, k - 1], rb3.at[part, k - 1], second(part, k)) for k in (1, 2, 3)],
        }

    sums = [scatter(0), scatter(1)]
    for part in (0, 1):
        product(part, 2)
        sums[part]["1p"].start()
        sums[part]["1m"].start()
    for part in (0, 1):
        product(part, 1)
        for k in (2, 3):
            sums[part]["2p"][k].start()
        product(part, 3)
        for k in (0, 1):
            sums[part]["2m"][k].start()

    def add(part, d1, k, got):
        ps[part, d1, k] = (ps[part, d1, k].astype(F32) + got[...].astype(F32)).astype(BF16)

    for part in (0, 1):
        sums[part]["1p"].wait_recv()
        for k in (1, 0):
            add(part, 1, k, rb1.at[part, 0, k])
            sums[part]["2p"][k].start()
        sums[part]["1m"].wait_recv()
        for k in (3, 2):
            add(part, 3, k, rb1.at[part, 1, k - 2])
            sums[part]["2m"][k].start()
    for part in (0, 1):
        product(part, 0)

    weights.whole(3)
    for n in range(4):
        weights.part(n)

    for k in (2, 3, 1, 0):
        for part in (0, 1):
            sums[part]["2p"][k].wait_recv()
            sums[part]["2m"][k].wait_recv()
            total = (
                ps[part, 0, k].astype(F32)
                + rb2[part, 0, k].astype(F32)
                + rb2[part, 1, k].astype(F32)
            )
            if k:
                qs[part, k - 1] = total.astype(BF16)
                sums[part]["3"][k - 1].start()
            else:
                merge_total[:, pl.ds(part * HALF, HALF)] = total

    for copy in halo_in:
        copy.wait_recv()
    local[2].wait()
    for w in range(3):
        h, r = normalize(xin[w].astype(F32))
        if w == 1:
            h_in[...] = h
            r_in[...] = r
        xin[w] = (h * ln_gain[...] + ln_bias[...]).astype(BF16)
    weights.finish()
    for j in range(3):
        for i in range(3):
            block = dot(xin[...].reshape(WINDOW, DV), qkv[:, pl.ds(j * DV + i * 384, 384)])
            t32[pl.ds(i * 384, 384), :] = block.T

        @pl.loop(0, HEADS)
        def _(n):
            cols = t32[pl.ds(pl.multiple_of(n * HD, 8), HD), :]
            heads[j * HEADS + n] = cols.astype(BF16)
            if j == 1:
                k_rows[n] = cols.T.astype(BF16)
            if j == 2:
                v_rows[n] = cols.T.astype(BF16)

    @pl.loop(0, HEADS)
    def _(n):
        scores = dot(k_rows[n], heads[n]) * SCALE
        allowed = id_col[...] == id_row[...]
        exponent = jnp.where(allowed, jnp.exp(jnp.where(allowed, scores, 0.0)), 0.0)
        denominator = jnp.sum(exponent, axis=0, keepdims=True) + 1.0 - live_row[...]
        weight = (exponent / denominator).astype(BF16)
        probs[n] = weight
        o_cols[n] = dot(heads[2 * HEADS + n], weight)

    for part in (0, 1):
        cols = pl.ds(part * HALF, HALF)
        for k in (2, 3, 1):
            sums[part]["3"][k - 1].wait_recv()
            merge_total[:, cols] += rb3[part, k - 1].astype(F32)
    for p in range(4):
        for t in range(9):
            strips[t, pl.ds(p, SLOTS, stride=4), :] = merge_total[:, pl.ds(DV * p + 128 * t, 128)]
    for t in range(9):
        wide[:, pl.ds(128 * t, 128)] = strips[t]
    og[1] = normalize_back(wide[...], h_out[...], r_out[...], merge_gain[...]).astype(BF16)
    halo_out = [
        copies.make(og.at[1], og.at[0], place.along(1)),
        copies.make(og.at[1], og.at[2], place.along(-1)),
    ]
    for copy in halo_out:
        copy.start()

    def project_back(w):
        for i in range(3):
            t32[pl.ds(i * 384, 384), pl.ds(w * PATCHES, PATCHES)] = dot(
                proj[pl.ds(i * 384, 384), :], og[w], NT
            )

    project_back(1)
    for w, copy in ((0, halo_out[0]), (2, halo_out[1])):
        copy.wait_recv()
        project_back(w)

    own = pl.ds(PATCHES, PATCHES)

    @pl.loop(0, HEADS)
    def _(n):
        start = pl.multiple_of(n * HD, 8)
        upstream = t32[pl.ds(start, HD), :].astype(BF16)
        delta = jnp.sum(upstream.astype(F32) * o_cols[n], axis=0, keepdims=True)
        prob1 = dot(v_rows[n], upstream[:, PATCHES : 2 * PATCHES])
        weight1 = probs[n, :, own].astype(F32)
        score1 = weight1 * (prob1 - delta[:, PATCHES : 2 * PATCHES]) * SCALE
        pg[pl.ds(start, HD), :] = dot(heads[HEADS + n], score1.astype(BF16))
        prob2 = dot(v_rows[n, own, :], upstream)
        weight2 = probs[n, own, :]
        score2 = (weight2.astype(F32) * (prob2 - delta) * SCALE).astype(BF16)
        pg[pl.ds(pl.multiple_of(start + DV, 8), HD), :] = dot(heads[n], score2, NT)
        pg[pl.ds(pl.multiple_of(start + 2 * DV, 8), HD), :] = dot(upstream, weight2, NT)

    projected_grad = pg[...].astype(BF16)
    for i in range(3):
        block = dot(qkv[pl.ds(i * 384, 384), :], projected_grad)
        wide[:, pl.ds(i * 384, 384)] = block.T
    out_ref[...] = (
        og[1].astype(F32) + normalize_back(wide[...], h_in[...], r_in[...], ln_gain[...])
    ).astype(BF16)
    copies.drain()


N_COPIES = 3 + 40 + 2 + 40 + 32 + 26 + 2


def local(
    grad_llm,
    vis_slot,
    image_rows,
    section_layer,
    vit_in,
    vit_out,
    ln_gain,
    ln_bias,
    qkv_weight,
    proj_weight,
    merge_gain,
    merge_bias,
    fc1_weight,
    fc1_bias,
    fc2_weight,
):
    s = lax.axis_index("section")
    v = lax.axis_index("vit")
    section_weight = jnp.where(
        section_layer < LEVELS, (section_layer + 1).astype(F32) / LEVELS, 0.0
    ).reshape(1, 4)
    counts = lax.dynamic_index_in_dim(image_rows, s, 0, keepdims=True)
    order = jnp.arange(16, dtype=jnp.int32)
    ends = jnp.sum(jnp.where(order[None, :] <= order[:, None], counts, 0), axis=1)
    total = jnp.sum(counts)
    slot_pos = lax.dynamic_slice_in_dim(vis_slot, s * 32, 32, 1).reshape(1, 512) - s * 512
    live_slot = (jnp.arange(512, dtype=jnp.int32) < total).astype(F32)[:, None]
    patch = v * PATCHES - PATCHES + jnp.arange(WINDOW, dtype=jnp.int32)
    slot = patch >> 2
    image = jnp.sum((slot[:, None] >= ends[None, :]).astype(jnp.int32), axis=1)
    live = (patch >= 0) & (slot < total)
    id_row = jnp.where(live, image, -1)[None, :]
    id_col = jnp.where(live, image, -2)[:, None]
    live_row = live.astype(F32)[None, :]

    anywhere = pl.BlockSpec(memory_space=pl.ANY)
    vmem = pl.BlockSpec(memory_space=pltpu.VMEM)
    smem = pl.BlockSpec(memory_space=pltpu.SMEM)

    def scratch(shape, dtype=BF16):
        return pltpu.VMEM(shape, dtype)

    return pl.pallas_call(
        body,
        out_shape=jax.ShapeDtypeStruct((PATCHES, DV), BF16),
        in_specs=[anywhere] * 7 + [smem] + [vmem] * 10,
        out_specs=vmem,
        scratch_shapes=[
            scratch((PATCHES, DV)),
            scratch((3, PATCHES, DV)),
            scratch((16, SLOTS, DM)),
            scratch((16, SLOTS, DL)),
            scratch((3, 32, DL)),
            scratch((32, DL)),
            scratch((HIDDEN, DM)),
            scratch((HIDDEN, DL)),
            scratch((DV, 3 * DV)),
            scratch((DV, DV)),
            scratch((PATCHES, DV), F32),
            scratch((PATCHES, 1), F32),
            scratch((PATCHES, DV), F32),
            scratch((PATCHES, 1), F32),
            scratch((PATCHES, DV), F32),
            scratch((512, HIDDEN), F32),
            scratch((512, HIDDEN), F32),
            scratch((16, SLOTS, HIDDEN)),
            scratch((2, 4, 4, SLOTS, HALF)),
            scratch((2, 2, 2, SLOTS, HALF)),
            scratch((2, 2, 4, SLOTS, HALF)),
            scratch((2, 3, SLOTS, HALF)),
            scratch((2, 3, SLOTS, HALF)),
            scratch((SLOTS, DM), F32),
            scratch((3, PATCHES, DV)),
            scratch((DV, WINDOW), F32),
            scratch((3 * HEADS, HD, WINDOW)),
            scratch((HEADS, WINDOW, HD)),
            scratch((HEADS, WINDOW, HD)),
            scratch((HEADS, WINDOW, WINDOW)),
            scratch((HEADS, HD, WINDOW), F32),
            scratch((3 * DV, PATCHES), F32),
            scratch((9, PATCHES, 128), F32),
            pltpu.SemaphoreType.DMA((N_COPIES,)),
            pltpu.SemaphoreType.DMA((N_COPIES,)),
            pltpu.SemaphoreType.DMA((7,)),
        ],
        compiler_params=pltpu.CompilerParams(
            collective_id=0, has_side_effects=True, vmem_limit_bytes=60 * 2**20
        ),
        name="merger_and_attention",
    )(
        grad_llm.reshape(grad_llm.shape[1:]),
        vit_in,
        vit_out,
        qkv_weight,
        proj_weight,
        fc1_weight.T,
        fc2_weight,
        section_weight,
        slot_pos,
        live_slot,
        id_row,
        id_col,
        live_row,
        ln_gain.reshape(1, DV),
        ln_bias.reshape(1, DV),
        merge_gain.reshape(1, DV),
        merge_bias.reshape(1, DV),
        fc1_bias.reshape(1, HIDDEN),
    )


def solution(mesh):
    placed = (
        P("section", ("dp", "vit"), None),
        P("dp", None),
        P("dp", None),
        P(),
        P(("dp", "section", "vit"), None),
        P(("dp", "section", "vit"), None),
        P(),
        P(),
        P("section", None),
        P("section", None),
        P(),
        P(),
        P(None, "vit"),
        P("vit"),
        P("vit", None),
    )
    return jax.shard_map(
        local,
        mesh=mesh,
        in_specs=placed,
        out_specs=P(("dp", "section", "vit"), None),
        check_vma=False,
    )
```

```python
import functools

import jax
import jax.numpy as jnp
from jax import lax
from jax.experimental import pallas as pl
from jax.experimental.pallas import tpu as pltpu
from jax.sharding import PartitionSpec as P

HEADS = 16
LEVELS = 3
DV = 1152
DM = 4608
DL = 4096
HD = 72
SLOTS = 32
PATCHES = 128
WINDOW = 384
HIDDEN = 288
HALF = DM // 2
SCALE = HD**-0.5
norm_eps = 1e-06
MESH = pl.DeviceIdType.MESH
F32 = jnp.float32
BF16 = jnp.bfloat16

NN = (((1,), (0,)), ((), ()))
NT = (((1,), (1,)), ((), ()))


def dot(a, b, dims=NN):
    return lax.dot_general(a, b, dims, preferred_element_type=F32)


def normalize(values):
    row_mean = jnp.mean(values, axis=-1, keepdims=True)
    centered = values - row_mean
    variance = jnp.mean(centered * centered, axis=-1, keepdims=True)
    inverse = lax.rsqrt(variance + norm_eps)
    return (centered * inverse, inverse)


def normalize_back(upstream, normed_rows, inverse, gain):
    scaled = upstream * gain
    mean_scaled = jnp.mean(scaled, axis=-1, keepdims=True)
    mean_cross = jnp.mean(scaled * normed_rows, axis=-1, keepdims=True)
    return (scaled - mean_scaled - normed_rows * mean_cross) * inverse


def gelu_slope(pre_act):
    cumulative = 0.5 * (1.0 + lax.erf(pre_act * 0.7071067811865476))
    density = jnp.exp(-0.5 * pre_act * pre_act) * 0.3989422804014327
    return cumulative + pre_act * density


class Place:
    def __init__(self):
        self.s = lax.axis_index("section")
        v = lax.axis_index("vit")
        d = lax.axis_index("dp")
        self.x, self.y = lax.rem(v, 4), v // 4
        self.c, self.zl = lax.rem(d, 2), d // 2
        self.z = self.s * 2 + self.zl
        self.v = v

    def at(self, dx=0, dy=0):
        x, y = lax.rem(self.x + dx + 4, 4), lax.rem(self.y + dy + 4, 4)
        return {"section": self.s, "vit": y * 4 + x, "dp": self.zl * 2 + self.c}

    def up(self, dz):
        z = lax.rem(self.z + dz + 8, 8)
        return {"section": z // 2, "vit": self.v, "dp": lax.rem(z, 2) * 2 + self.c}

    def other_core(self):
        return {"section": self.s, "vit": self.v, "dp": self.zl * 2 + 1 - self.c}

    def along(self, dv):
        return {"section": self.s, "vit": lax.rem(self.v + dv + 16, 16), "dp": self.zl * 2 + self.c}


class Copies:
    def __init__(self, ssem, rsem):
        self.ssem, self.rsem, self.made, self.count = ssem, rsem, [], 0

    def make(self, src, dst, device, drained=True):
        k = self.count
        self.count += 1
        copy = pltpu.make_async_remote_copy(
            src, dst, self.ssem.at[k], self.rsem.at[k], device_id=device, device_id_type=MESH
        )
        if drained:
            self.made.append(copy)
        return copy

    def drain(self):
        for copy in self.made:
            copy.wait_send()


class PlaneGather:
    def __init__(self, place, copies, buf, width, split):
        self.parts = []
        for axis in (0, 1):
            cols = pl.ds(0, split) if axis == 0 else pl.ds(split, width - split)

            def block(d1, d2, axis=axis):
                dx, dy = (d1, d2) if axis == 0 else (d2, d1)
                return lax.rem(place.y + dy + 4, 4) * 4 + lax.rem(place.x + dx + 4, 4)

            def first(d, axis=axis):
                return place.at(d, 0) if axis == 0 else place.at(0, d)

            def second(d, axis=axis):
                return place.at(0, d) if axis == 0 else place.at(d, 0)

            def send(d1, d2, rows, device, block=block, cols=cols):
                ref = buf.at[block(d1, d2), rows, cols]
                return copies.make(ref, ref, device)

            every, low, high = pl.ds(0, 32), pl.ds(0, 16), pl.ds(16, 16)
            part = {
                "s1p": send(0, 0, every, first(1)),
                "s1m": send(0, 0, every, first(-1)),
                "f1p": send(-1, 0, low, first(1)),
                "f1m": send(1, 0, high, first(-1)),
            }
            for d1 in (0, -1, 1, 2):
                part["s2p", d1] = send(d1, 0, every, second(1))
                part["s2m", d1] = send(d1, 0, every, second(-1))
                part["f2p", d1] = send(d1, -1, low, second(1))
                part["f2m", d1] = send(d1, 1, high, second(-1))
            self.parts.append(part)

    def start(self):
        for p in self.parts:
            for k in ("s1p", "s1m", ("s2p", 0), ("s2m", 0)):
                p[k].start()

    def near(self):
        for p in self.parts:
            p["s1p"].wait_recv()
            p["f1p"].start()
            p["s2p", -1].start()
            p["s2m", -1].start()
            p["s1m"].wait_recv()
            p["f1m"].start()
            p["s2p", 1].start()
            p["s2m", 1].start()

    def far(self):
        for p in self.parts:
            p["f1p"].wait_recv()
            p["f1m"].wait_recv()
            p["s2p", 2].start()
            p["s2m", 2].start()

    def pass_on(self, d1):
        for p in self.parts:
            p["s2p", d1].wait_recv()
            p["f2p", d1].start()
            p["s2m", d1].wait_recv()
            p["f2m", d1].start()

    def finish(self):
        for d1 in (0, -1, 1, 2):
            for p in self.parts:
                p["f2p", d1].wait_recv()
                p["f2m", d1].wait_recv()


class WeightGather:
    def __init__(self, place, copies, qkv, proj):
        s, c, zl = place.s, place.c, place.zl
        self.odd = zl == 1
        self.even = zl == 0
        chunks = [
            (qkv, 48, n * 48, 3456, 1792) for n in range(3)
        ] + [(proj, 144, 0, 1152, 640)]

        def piece(chunk, section, side):
            ref, rows, offset, width, split = chunk
            start = pl.multiple_of(lax.rem(section + 8, 4) * 288 + c * 144 + offset, 16)
            cols = {
                0: pl.ds(0, width), 1: pl.ds(0, split), 2: pl.ds(split, width - split)
            }[side]
            return ref.at[pl.ds(start, rows), cols]

        def make(chunk, section, side, device, drained=True):
            ref = piece(chunk, section, side)
            return copies.make(ref, ref, device, drained)

        right, left, core = place.up(1), place.up(-1), place.other_core()
        self.right, self.left = [], []
        for ch in chunks:
            self.right.append((
                make(ch, s - 1 + zl, 0, right, False),
                make(ch, s - 1, 0, core),
                make(ch, s - 2 + zl, 1, right),
                make(ch, s - 2, 1, core),
            ))
            self.left.append((
                make(ch, s + zl, 0, left, False),
                make(ch, s + 1, 0, core),
                make(ch, s + zl + 1, 2, left),
                make(ch, s + 2, 2, core),
            ))

    def each(self):
        return ((self.odd, self.even, self.right), (self.even, self.odd, self.left))

    def start(self):
        for lead, _, side in self.each():
            pl.when(lead)(side[0][0].start)

    def follow_whole(self, n):
        for lead, follow, side in self.each():
            whole, core, _, _ = side[n]
            if n < 3:

                @pl.when(lead)
                def _():
                    whole.wait_send()
                    side[n + 1][0].start()

            @pl.when(follow)
            def _():
                whole.wait_recv()
                core.start()
                whole.start()

    def lead_whole(self, n):
        for lead, _, side in self.each():
            whole, core, part, _ = side[n]

            @pl.when(lead)
            def _():
                whole.wait_recv()
                core.start()
                part.start()

    def follow_part(self, n):
        for _, follow, side in self.each():
            _, _, part, core = side[n]

            @pl.when(follow)
            def _():
                part.wait_recv()
                core.start()
                part.start()

    def lead_part(self, n):
        for lead, _, side in self.each():
            _, _, part, core = side[n]

            @pl.when(lead)
            def _():
                part.wait_recv()
                core.start()

    def step(self, k):
        for n, act in (
            (k, self.follow_whole), (k - 1, self.lead_whole), (k - 2, self.follow_part), (k - 3, self.lead_part)
        ):
            if 0 <= n < 4:
                act(n)

    def finish(self, pieces):
        for side in (self.right, self.left):
            for n in pieces:
                side[n][1].wait_recv()
                side[n][3].wait_recv()

    def drain(self):
        for _, follow, side in self.each():
            for n in range(3):
                pl.when(follow)(side[n][0].wait_send)
            side[3][0].wait_send()


def body(
    grad, vit_in, vit_out, qkv_w, proj_w, fc1_w, fc2_w,
    ln_gain_h, ln_bias_h, merge_gain_h, merge_bias_h, fc1_bias_h, vis_slot_h,
    image_rows, section_layer,
    out_ref,
    xo, xin, rows_in, rows_grad, zin, zown, fc1, fc2, qkv, proj,
    h_out, r_out, h_in, r_in, wide, slope, hidden, pre_grad,
    ps, rb1, rb2, qs, rb3, merge_total, og,
    t32, heads, k_rows, v_rows, probs, o_cols, pg, strips,
    ln_gain_v, ln_bias_v, merge_gain_v, merge_bias_v, fc1_bias_v, vis_slot, ssem, rsem, lsem,
):
    place = Place()
    s, x, y = place.s, place.x, place.y
    copies = Copies(ssem, rsem)

    near = [place.at(1, 0), place.at(-1, 0), place.at(2, 0), place.at(0, 1), place.at(0, -1), place.at(0, 2)]
    near += [place.up(1), place.up(-1), place.up(2), place.up(-2), place.up(4), place.other_core()]
    near += [place.along(1), place.along(-1)]
    barrier = pltpu.get_barrier_semaphore()
    for device in near:
        pl.semaphore_signal(barrier, inc=1, device_id=device, device_id_type=MESH)

    own_rows = pl.ds(pl.multiple_of(s * 288, 16), 288)
    group_rows = pl.ds(pl.multiple_of(s * 32, 32), 32)
    local = [
        pltpu.make_async_copy(src, dst, lsem.at[k])
        for k, (src, dst) in enumerate((
            (vit_out, xo),
            (grad.at[group_rows], zown),
            (vit_in, xin.at[1]),
            (fc1_w, fc1),
            (qkv_w, qkv.at[own_rows]),
            (proj_w, proj.at[own_rows]),
            (fc2_w, fc2),
            (merge_gain_h, merge_gain_v),
            (merge_bias_h, merge_bias_v),
            (ln_gain_h, ln_gain_v),
            (ln_bias_h, ln_bias_v),
            (fc1_bias_h, fc1_bias_v),
            (vis_slot_h, vis_slot),
        ))
    ]
    for k in (0, 7, 8, 1, 4, 5, 3, 6, 2, 9, 10, 11, 12):
        local[k].start()

    me = place.v
    for k in (0, 7, 8):
        local[k].wait()
    merge_gain = merge_gain_v[...].reshape(1, DV)
    merge_bias = merge_bias_v[...].reshape(1, DV)
    h, r = normalize(xo[...].astype(F32))
    h_out[...] = h
    r_out[...] = r
    value = h * merge_gain + merge_bias
    for t in range(9):
        strips[t] = value[:, 128 * t : 128 * t + 128]
    for p in range(4):
        for t in range(9):
            strip = strips[t, pl.ds(p, SLOTS, stride=4), :]
            rows_in[me, :, pl.ds(DV * p + 128 * t, 128)] = strip.astype(BF16)

    pl.semaphore_wait(barrier, len(near))

    z_copies = []
    for d in (1, 2, 3):
        rows = pl.ds(pl.multiple_of(lax.rem(s + d, 4) * 32, 32), 32)
        z_copies.append(copies.make(grad.at[rows], zin.at[d - 1], place.up(2 * d)))
    for copy in (z_copies[0], z_copies[2], z_copies[1]):
        copy.start()
    gather_in = PlaneGather(place, copies, rows_in, DM, HALF)
    gather_in.start()
    halo_in = [
        copies.make(vit_in, xin.at[0], place.along(1)),
        copies.make(vit_in, xin.at[2], place.along(-1)),
    ]
    gather_grad = PlaneGather(place, copies, rows_grad, DL, DL // 2)
    weights = WeightGather(place, copies, qkv, proj)
    for k in (4, 5):
        local[k].wait()
    weights.start()

    gather_in.near()
    gather_in.pass_on(0)
    gather_in.far()
    gather_in.pass_on(-1)
    gather_in.pass_on(1)
    weights.step(0)
    gather_in.pass_on(2)
    local[1].wait()
    for copy in z_copies:
        copy.wait_recv()

    level = [section_layer[lax.rem(s + 4 - d, 4)] for d in range(4)]
    level = [
        jnp.where(n == 0, 1 / 3, jnp.where(n == 1, 2 / 3, jnp.where(n == 2, 1.0, 0.0))).astype(F32)
        for n in level
    ]

    @pl.loop(0, 4)
    def _(i):
        cols = pl.ds(pl.multiple_of(i * 1024, 128), 1024)
        total = level[0] * zown[:, cols].astype(F32)
        for d in (1, 2, 3):
            total += level[d] * zin[d - 1, :, cols].astype(F32)
        rows_grad[me, :, cols] = total.astype(BF16)

    gather_grad.start()
    for copy in halo_in:
        copy.start()
    weights.step(1)
    gather_in.finish()
    for k in (3, 11):
        local[k].wait()
    fc1_bias = fc1_bias_v[...].reshape(1, HIDDEN)

    def fill_slope(lo, hi):
        @pl.loop(lo, hi)
        def _(i):
            block = rows_in[pl.ds(i * 4, 4)].reshape(128, DM)
            rows = pl.ds(pl.multiple_of(i * 128, 128), 128)
            slope[rows, :] = gelu_slope(dot(block, fc1[...], NT) + fc1_bias)

    gather_grad.near()
    fill_slope(0, 2)
    weights.step(2)
    gather_grad.pass_on(0)
    gather_grad.far()
    fill_slope(2, 4)
    weights.step(3)
    gather_grad.pass_on(-1)
    gather_grad.pass_on(1)
    weights.step(4)
    gather_grad.pass_on(2)
    for k in (2, 6, 9, 10, 12):
        local[k].wait()
    gather_grad.finish()

    @pl.loop(0, 4)
    def _(i):
        block = rows_grad[pl.ds(i * 4, 4)].reshape(128, DL)
        rows = pl.ds(pl.multiple_of(i * 128, 128), 128)
        hidden[rows, :] = dot(block, fc2[...], NT)


    weights.step(5)

    ends = []
    for k in range(16):
        count = image_rows[s, k]
        ends.append(count if k == 0 else ends[-1] + count)
    total_slots = ends[-1]

    shifted = [pltpu.roll(vis_slot[...], lax.rem(32 * q + 128 - 32 * s, 128), 1) for q in range(4)]
    quarter = lax.broadcasted_iota(jnp.int32, (1, 128), 1) // 32
    positions = []
    for t in range(4):
        position = shifted[0][4 * t : 4 * t + 1, :]
        for q in (1, 2, 3):
            position = jnp.where(quarter == q, shifted[q][4 * t + q : 4 * t + q + 1, :], position)
        positions.append(position - 512 * s)
    value = hidden[...]
    high = value.astype(BF16)
    low = (value - high.astype(F32)).astype(BF16)
    for i in range(4):
        slots = lax.broadcasted_iota(jnp.int32, (128, 128), 0) + 128 * i
        placed = jnp.zeros((128, HIDDEN), F32)
        for t in range(4):
            chosen = jnp.where(slots == positions[t], 1.0, 0.0).astype(BF16)
            from_rows = slice(128 * t, 128 * t + 128)
            placed += dot(chosen, high[from_rows]) + dot(chosen, low[from_rows])
        live = lax.broadcasted_iota(jnp.int32, (128, HIDDEN), 0) + 128 * i < total_slots
        block = jnp.where(live, placed, 0.0) * slope[pl.ds(128 * i, 128), :]
        pre_grad[pl.ds(4 * i, 4)] = block.astype(BF16).reshape(4, SLOTS, HIDDEN)

    def token(part, d1, d2):
        dx, dy = (d1, d2) if part == 0 else (d2, d1)
        return lax.rem(y + dy, 4) * 4 + lax.rem(x + dx, 4)

    def first(part, d):
        return place.at(d, 0) if part == 0 else place.at(0, d)

    def second(part, d):
        return place.at(0, d) if part == 0 else place.at(d, 0)

    def product(part, d1):
        block = jnp.concatenate([pre_grad[token(part, d1, d2)] for d2 in range(4)], axis=0)

        @pl.loop(0, 6)
        def _(i):
            start = pl.multiple_of(i * 384, 128)
            cols = pl.ds(pl.multiple_of(start + part * HALF, 128), 384)
            term = dot(block, fc1[:, cols]).astype(BF16).reshape(4, SLOTS, 384)
            ps[part, d1, :, :, pl.ds(start, 384)] = term

    def scatter(part):
        low, high = pl.ds(0, 2), pl.ds(2, 2)
        near1, near2 = first(part, 1), first(part, -1)
        return {
            "1p": copies.make(ps.at[part, 2, low], rb1.at[part, 0], near1),
            "1m": copies.make(ps.at[part, 2, high], rb1.at[part, 1], near2),
            "2p": [copies.make(ps.at[part, 1, k], rb2.at[part, 0, k], near1) for k in range(4)],
            "2m": [copies.make(ps.at[part, 3, k], rb2.at[part, 1, k], near2) for k in range(4)],
            "3": [copies.make(qs.at[part, k - 1], rb3.at[part, k - 1], second(part, k)) for k in (1, 2, 3)],
        }

    sums = [scatter(0), scatter(1)]
    for part in (0, 1):
        product(part, 2)
        sums[part]["1p"].start()
        sums[part]["1m"].start()
    for part in (0, 1):
        product(part, 1)
        for k in (2, 3):
            sums[part]["2p"][k].start()
        product(part, 3)
        for k in (0, 1):
            sums[part]["2m"][k].start()

    def add(part, d1, k, got):
        ps[part, d1, k] = (ps[part, d1, k].astype(F32) + got[...].astype(F32)).astype(BF16)

    for part in (0, 1):
        sums[part]["1p"].wait_recv()
        for k in (1, 0):
            add(part, 1, k, rb1.at[part, 0, k])
            sums[part]["2p"][k].start()
        sums[part]["1m"].wait_recv()
        for k in (3, 2):
            add(part, 3, k, rb1.at[part, 1, k - 2])
            sums[part]["2m"][k].start()
    for part in (0, 1):
        product(part, 0)

    weights.step(6)
    for copy in halo_in:
        copy.wait_recv()
    ln_gain = ln_gain_v[...].reshape(1, DV)
    ln_bias = ln_bias_v[...].reshape(1, DV)

    for w in range(3):
        h, r = normalize(xin[w].astype(F32))
        if w == 1:
            h_in[...] = h
            r_in[...] = r
        xin[w] = (h * ln_gain + ln_bias).astype(BF16)

    def attend(j):
        for i in range(3):
            block = dot(xin[...].reshape(WINDOW, DV), qkv[:, pl.ds(j * DV + i * 384, 384)])
            t32[pl.ds(i * 384, 384), :] = block.T

        @pl.loop(0, HEADS, unroll=2)
        def _(n):
            cols = t32[pl.ds(pl.multiple_of(n * HD, 8), HD), :]
            heads[j * HEADS + n] = cols.astype(BF16)
            if j == 1:
                k_rows[n] = cols.T.astype(BF16)
            if j == 2:
                v_rows[n] = cols.T.astype(BF16)

    weights.finish((0, 1, 2))
    attend(0)
    for k in (2, 3, 1, 0):
        for part in (0, 1):
            sums[part]["2p"][k].wait_recv()
            sums[part]["2m"][k].wait_recv()
            total = (
                ps[part, 0, k].astype(F32)
                + rb2[part, 0, k].astype(F32)
                + rb2[part, 1, k].astype(F32)
            )
            if k:
                qs[part, k - 1] = total.astype(BF16)
                sums[part]["3"][k - 1].start()
            else:
                merge_total[:, pl.ds(part * HALF, HALF)] = total
    attend(1)
    attend(2)

    def image_of(axis):
        shape = (1, WINDOW) if axis else (WINDOW, 1)
        patch = lax.broadcasted_iota(jnp.int32, shape, axis) + (place.v * PATCHES - PATCHES)
        slot = patch >> 2
        image = jnp.zeros(shape, jnp.int32)
        for end in ends:
            image += jnp.where(slot >= end, 1, 0)
        live = (patch >= 0) & (slot < total_slots)
        return jnp.where(live, image, axis - 2), live

    id_row, live_row = image_of(1)
    id_col, _ = image_of(0)
    dead_row = jnp.where(live_row, 0.0, 1.0)

    @pl.loop(0, HEADS, unroll=2)
    def _(n):
        scores = dot(k_rows[n], heads[n]) * SCALE
        allowed = id_col == id_row
        exponent = jnp.where(allowed, jnp.exp(jnp.where(allowed, scores, 0.0)), 0.0)
        denominator = jnp.sum(exponent, axis=0, keepdims=True) + dead_row
        weight = (exponent / denominator).astype(BF16)
        probs[n] = weight
        o_cols[n] = dot(heads[2 * HEADS + n], weight)

    for part in (0, 1):
        cols = pl.ds(part * HALF, HALF)
        for k in (2, 3, 1):
            sums[part]["3"][k - 1].wait_recv()
            merge_total[:, cols] += rb3[part, k - 1].astype(F32)
    for p in range(4):
        for t in range(9):
            strips[t, pl.ds(p, SLOTS, stride=4), :] = merge_total[:, pl.ds(DV * p + 128 * t, 128)]
    for t in range(9):
        wide[:, pl.ds(128 * t, 128)] = strips[t]
    og[1] = normalize_back(wide[...], h_out[...], r_out[...], merge_gain).astype(BF16)
    halo_out = [
        copies.make(og.at[1], og.at[0], place.along(1)),
        copies.make(og.at[1], og.at[2], place.along(-1)),
    ]
    for copy in halo_out:
        copy.start()

    def project_back(w):
        for i in range(3):
            t32[pl.ds(i * 384, 384), pl.ds(w * PATCHES, PATCHES)] = dot(
                proj[pl.ds(i * 384, 384), :], og[w], NT
            )

    weights.finish((3,))
    project_back(1)
    for w, copy in ((0, halo_out[0]), (2, halo_out[1])):
        copy.wait_recv()
        project_back(w)

    own = pl.ds(PATCHES, PATCHES)

    @pl.loop(0, HEADS, unroll=2)
    def _(n):
        start = pl.multiple_of(n * HD, 8)
        upstream = t32[pl.ds(start, HD), :].astype(BF16)
        delta = jnp.sum(upstream.astype(F32) * o_cols[n], axis=0, keepdims=True)
        prob1 = dot(v_rows[n], upstream[:, PATCHES : 2 * PATCHES])
        weight1 = probs[n, :, own].astype(F32)
        score1 = weight1 * (prob1 - delta[:, PATCHES : 2 * PATCHES]) * SCALE
        pg[pl.ds(start, HD), :] = dot(heads[HEADS + n], score1.astype(BF16))
        prob2 = dot(v_rows[n, own, :], upstream)
        weight2 = probs[n, own, :]
        score2 = (weight2.astype(F32) * (prob2 - delta) * SCALE).astype(BF16)
        pg[pl.ds(pl.multiple_of(start + DV, 8), HD), :] = dot(heads[n], score2, NT)
        pg[pl.ds(pl.multiple_of(start + 2 * DV, 8), HD), :] = dot(upstream, weight2, NT)

    projected_grad = pg[...].astype(BF16)
    for i in range(3):
        block = dot(qkv[pl.ds(i * 384, 384), :], projected_grad)
        wide[:, pl.ds(i * 384, 384)] = block.T
    out_ref[...] = (
        og[1].astype(F32) + normalize_back(wide[...], h_in[...], r_in[...], ln_gain)
    ).astype(BF16)
    copies.drain()
    weights.drain()


N_COPIES = 3 + 40 + 2 + 40 + 32 + 26 + 2


def local(
    grad_llm,
    vis_slot,
    image_rows,
    section_layer,
    vit_in,
    vit_out,
    ln_gain,
    ln_bias,
    qkv_weight,
    proj_weight,
    merge_gain,
    merge_bias,
    fc1_weight,
    fc1_bias,
    fc2_weight,
):
    anywhere = pl.BlockSpec(memory_space=pl.ANY)
    vmem = pl.BlockSpec(memory_space=pltpu.VMEM)
    smem = pl.BlockSpec(memory_space=pltpu.SMEM)

    def scratch(shape, dtype=BF16):
        return pltpu.VMEM(shape, dtype)

    return pl.pallas_call(
        body,
        out_shape=jax.ShapeDtypeStruct((PATCHES, DV), BF16),
        in_specs=[anywhere] * 13 + [smem] * 2,
        out_specs=vmem,
        scratch_shapes=[
            scratch((PATCHES, DV)),
            scratch((3, PATCHES, DV)),
            scratch((16, SLOTS, DM)),
            scratch((16, SLOTS, DL)),
            scratch((3, 32, DL)),
            scratch((32, DL)),
            scratch((HIDDEN, DM)),
            scratch((HIDDEN, DL)),
            scratch((DV, 3 * DV)),
            scratch((DV, DV)),
            scratch((PATCHES, DV), F32),
            scratch((PATCHES, 1), F32),
            scratch((PATCHES, DV), F32),
            scratch((PATCHES, 1), F32),
            scratch((PATCHES, DV), F32),
            scratch((512, HIDDEN), F32),
            scratch((512, HIDDEN), F32),
            scratch((16, SLOTS, HIDDEN)),
            scratch((2, 4, 4, SLOTS, HALF)),
            scratch((2, 2, 2, SLOTS, HALF)),
            scratch((2, 2, 4, SLOTS, HALF)),
            scratch((2, 3, SLOTS, HALF)),
            scratch((2, 3, SLOTS, HALF)),
            scratch((SLOTS, DM), F32),
            scratch((3, PATCHES, DV)),
            scratch((DV, WINDOW), F32),
            scratch((3 * HEADS, HD, WINDOW)),
            scratch((HEADS, WINDOW, HD)),
            scratch((HEADS, WINDOW, HD)),
            scratch((HEADS, WINDOW, WINDOW)),
            scratch((HEADS, HD, WINDOW), F32),
            scratch((3 * DV, PATCHES), F32),
            scratch((9, PATCHES, 128), F32),
            scratch((DV,), F32),
            scratch((DV,), F32),
            scratch((DV,), F32),
            scratch((DV,), F32),
            scratch((HIDDEN,), F32),
            scratch((16, 128), jnp.int32),
            pltpu.SemaphoreType.DMA((N_COPIES,)),
            pltpu.SemaphoreType.DMA((N_COPIES,)),
            pltpu.SemaphoreType.DMA((13,)),
        ],
        compiler_params=pltpu.CompilerParams(
            collective_id=0, has_side_effects=True, vmem_limit_bytes=60 * 2**20
        ),
        name="merger_and_attention",
    )(
        grad_llm.reshape(grad_llm.shape[1:]),
        vit_in,
        vit_out,
        qkv_weight,
        proj_weight,
        fc1_weight.T,
        fc2_weight,
        ln_gain,
        ln_bias,
        merge_gain,
        merge_bias,
        fc1_bias,
        vis_slot,
        image_rows,
        section_layer,
    )


def solution(mesh):
    placed = (
        P("section", ("dp", "vit"), None),
        P("dp", None),
        P("dp", None),
        P(),
        P(("dp", "section", "vit"), None),
        P(("dp", "section", "vit"), None),
        P(),
        P(),
        P("section", None),
        P("section", None),
        P(),
        P(),
        P(None, "vit"),
        P("vit"),
        P("vit", None),
    )
    return jax.shard_map(
        local,
        mesh=mesh,
        in_specs=placed,
        out_specs=P(("dp", "section", "vit"), None),
        check_vma=False,
    )
```

```python
import functools

import jax
import jax.numpy as jnp
from jax import lax
from jax.experimental import pallas as pl
from jax.experimental.pallas import tpu as pltpu
from jax.sharding import PartitionSpec as P

HEADS = 16
LEVELS = 3
DV = 1152
DM = 4608
DL = 4096
HD = 72
SLOTS = 32
PATCHES = 128
WINDOW = 384
HIDDEN = 288
HALF = DM // 2
SCALE = HD**-0.5
norm_eps = 1e-06
MESH = pl.DeviceIdType.MESH
F32 = jnp.float32
BF16 = jnp.bfloat16

NN = (((1,), (0,)), ((), ()))
NT = (((1,), (1,)), ((), ()))


def dot(a, b, dims=NN):
    return lax.dot_general(a, b, dims, preferred_element_type=F32)


def normalize(values):
    row_mean = jnp.mean(values, axis=-1, keepdims=True)
    centered = values - row_mean
    variance = jnp.mean(centered * centered, axis=-1, keepdims=True)
    inverse = lax.rsqrt(variance + norm_eps)
    return (centered * inverse, inverse)


def normalize_back(upstream, normed_rows, inverse, gain):
    scaled = upstream * gain
    mean_scaled = jnp.mean(scaled, axis=-1, keepdims=True)
    mean_cross = jnp.mean(scaled * normed_rows, axis=-1, keepdims=True)
    return (scaled - mean_scaled - normed_rows * mean_cross) * inverse


def gelu_slope(pre_act):
    cumulative = 0.5 * (1.0 + lax.erf(pre_act * 0.7071067811865476))
    density = jnp.exp(-0.5 * pre_act * pre_act) * 0.3989422804014327
    return cumulative + pre_act * density


class Place:
    def __init__(self):
        self.s = lax.axis_index("section")
        v = lax.axis_index("vit")
        d = lax.axis_index("dp")
        self.x, self.y = lax.rem(v, 4), v // 4
        self.c, self.zl = lax.rem(d, 2), d // 2
        self.z = self.s * 2 + self.zl
        self.v = v

    def at(self, dx=0, dy=0):
        x, y = lax.rem(self.x + dx + 4, 4), lax.rem(self.y + dy + 4, 4)
        return {"section": self.s, "vit": y * 4 + x, "dp": self.zl * 2 + self.c}

    def up(self, dz):
        z = lax.rem(self.z + dz + 8, 8)
        return {"section": z // 2, "vit": self.v, "dp": lax.rem(z, 2) * 2 + self.c}

    def other_core(self):
        return {"section": self.s, "vit": self.v, "dp": self.zl * 2 + 1 - self.c}

    def along(self, dv):
        return {"section": self.s, "vit": lax.rem(self.v + dv + 16, 16), "dp": self.zl * 2 + self.c}


class Copies:
    def __init__(self, ssem, rsem):
        self.ssem, self.rsem, self.made, self.count = ssem, rsem, [], 0

    def make(self, src, dst, device, drained=True):
        k = self.count
        self.count += 1
        copy = pltpu.make_async_remote_copy(
            src, dst, self.ssem.at[k], self.rsem.at[k], device_id=device, device_id_type=MESH
        )
        if drained:
            self.made.append(copy)
        return copy

    def drain(self):
        for copy in self.made:
            copy.wait_send()


class PlaneGather:
    def __init__(self, place, copies, buf, width, split):
        self.parts = []
        for axis in (0, 1):
            cols = pl.ds(0, split) if axis == 0 else pl.ds(split, width - split)

            def block(d1, d2, axis=axis):
                dx, dy = (d1, d2) if axis == 0 else (d2, d1)
                return lax.rem(place.y + dy + 4, 4) * 4 + lax.rem(place.x + dx + 4, 4)

            def first(d, axis=axis):
                return place.at(d, 0) if axis == 0 else place.at(0, d)

            def second(d, axis=axis):
                return place.at(0, d) if axis == 0 else place.at(d, 0)

            def send(d1, d2, rows, device, block=block, cols=cols):
                ref = buf.at[block(d1, d2), rows, cols]
                return copies.make(ref, ref, device)

            every, low, high = pl.ds(0, 32), pl.ds(0, 16), pl.ds(16, 16)
            part = {
                "s1p": send(0, 0, every, first(1)),
                "s1m": send(0, 0, every, first(-1)),
                "f1p": send(-1, 0, low, first(1)),
                "f1m": send(1, 0, high, first(-1)),
            }
            for d1 in (0, -1, 1, 2):
                part["s2p", d1] = send(d1, 0, every, second(1))
                part["s2m", d1] = send(d1, 0, every, second(-1))
                part["f2p", d1] = send(d1, -1, low, second(1))
                part["f2m", d1] = send(d1, 1, high, second(-1))
            self.parts.append(part)

    def start(self):
        for p in self.parts:
            for k in ("s1p", "s1m", ("s2p", 0), ("s2m", 0)):
                p[k].start()

    def near(self):
        for p in self.parts:
            p["s1p"].wait_recv()
            p["f1p"].start()
            p["s2p", -1].start()
            p["s2m", -1].start()
            p["s1m"].wait_recv()
            p["f1m"].start()
            p["s2p", 1].start()
            p["s2m", 1].start()

    def far(self):
        for p in self.parts:
            p["f1p"].wait_recv()
            p["f1m"].wait_recv()
            p["s2p", 2].start()
            p["s2m", 2].start()

    def pass_on(self, d1):
        for p in self.parts:
            p["s2p", d1].wait_recv()
            p["f2p", d1].start()
            p["s2m", d1].wait_recv()
            p["f2m", d1].start()

    def finish(self):
        for d1 in (0, -1, 1, 2):
            for p in self.parts:
                p["f2p", d1].wait_recv()
                p["f2m", d1].wait_recv()


class WeightGather:
    def __init__(self, place, copies, qkv, proj):
        s, c, zl = place.s, place.c, place.zl
        self.odd = zl == 1
        self.even = zl == 0
        chunks = [
            (qkv, 48, n * 48, 3456, 1792) for n in range(3)
        ] + [(proj, 144, 0, 1152, 640)]

        def piece(chunk, section, side):
            ref, rows, offset, width, split = chunk
            start = pl.multiple_of(lax.rem(section + 8, 4) * 288 + c * 144 + offset, 16)
            cols = {
                0: pl.ds(0, width), 1: pl.ds(0, split), 2: pl.ds(split, width - split)
            }[side]
            return ref.at[pl.ds(start, rows), cols]

        def make(chunk, section, side, device, drained=True):
            ref = piece(chunk, section, side)
            return copies.make(ref, ref, device, drained)

        right, left, core = place.up(1), place.up(-1), place.other_core()
        self.right, self.left = [], []
        for ch in chunks:
            self.right.append((
                make(ch, s - 1 + zl, 0, right, False),
                make(ch, s - 1, 0, core),
                make(ch, s - 2 + zl, 1, right),
                make(ch, s - 2, 1, core),
            ))
            self.left.append((
                make(ch, s + zl, 0, left, False),
                make(ch, s + 1, 0, core),
                make(ch, s + zl + 1, 2, left),
                make(ch, s + 2, 2, core),
            ))

    def each(self):
        return ((self.odd, self.even, self.right), (self.even, self.odd, self.left))

    def start(self):
        for lead, _, side in self.each():
            pl.when(lead)(side[0][0].start)

    def follow_whole(self, n):
        for lead, follow, side in self.each():
            whole, core, _, _ = side[n]
            if n < 3:

                @pl.when(lead)
                def _():
                    whole.wait_send()
                    side[n + 1][0].start()

            @pl.when(follow)
            def _():
                whole.wait_recv()
                core.start()
                whole.start()

    def lead_whole(self, n):
        for lead, _, side in self.each():
            whole, core, part, _ = side[n]

            @pl.when(lead)
            def _():
                whole.wait_recv()
                core.start()
                part.start()

    def follow_part(self, n):
        for _, follow, side in self.each():
            _, _, part, core = side[n]

            @pl.when(follow)
            def _():
                part.wait_recv()
                core.start()
                part.start()

    def lead_part(self, n):
        for lead, _, side in self.each():
            _, _, part, core = side[n]

            @pl.when(lead)
            def _():
                part.wait_recv()
                core.start()

    def step(self, k):
        for n, act in (
            (k, self.follow_whole), (k - 1, self.lead_whole), (k - 2, self.follow_part), (k - 3, self.lead_part)
        ):
            if 0 <= n < 4:
                act(n)

    def finish(self, pieces):
        for side in (self.right, self.left):
            for n in pieces:
                side[n][1].wait_recv()
                side[n][3].wait_recv()

    def drain(self):
        for _, follow, side in self.each():
            for n in range(3):
                pl.when(follow)(side[n][0].wait_send)
            side[3][0].wait_send()


def body(
    grad, vit_in, vit_out, qkv_w, proj_w, fc1_w, fc2_w,
    ln_gain_h, ln_bias_h, merge_gain_h, merge_bias_h, fc1_bias_h, vis_slot_h,
    image_rows, section_layer,
    out_ref,
    xo, xin, rows_in, rows_grad, zin, zown, fc1, fc2, qkv, proj,
    h_out, r_out, h_in, r_in, wide, slope, hidden, pre_grad,
    ps, rb1, rb2, qs, rb3, merge_total, og,
    t32, heads, k_rows, v_rows, probs, o_cols, pg, strips,
    ln_gain_v, ln_bias_v, merge_gain_v, merge_bias_v, fc1_bias_v, vis_slot, ssem, rsem, lsem,
):
    place = Place()
    s, x, y = place.s, place.x, place.y
    copies = Copies(ssem, rsem)

    near = [place.at(1, 0), place.at(-1, 0), place.at(2, 0), place.at(0, 1), place.at(0, -1), place.at(0, 2)]
    near += [place.up(1), place.up(-1), place.up(2), place.up(-2), place.up(4), place.other_core()]
    near += [place.along(1), place.along(-1)]
    barrier = pltpu.get_barrier_semaphore()
    for device in near:
        pl.semaphore_signal(barrier, inc=1, device_id=device, device_id_type=MESH)

    own_rows = pl.ds(pl.multiple_of(s * 288, 16), 288)
    group_rows = pl.ds(pl.multiple_of(s * 32, 32), 32)
    local = [
        pltpu.make_async_copy(src, dst, lsem.at[k])
        for k, (src, dst) in enumerate((
            (vit_out, xo),
            (grad.at[group_rows], zown),
            (vit_in, xin.at[0]),
            (fc1_w, fc1),
            (qkv_w, qkv.at[own_rows]),
            (proj_w, proj.at[own_rows]),
            (fc2_w, fc2),
            (merge_gain_h, merge_gain_v),
            (merge_bias_h, merge_bias_v),
            (ln_gain_h, ln_gain_v),
            (ln_bias_h, ln_bias_v),
            (fc1_bias_h, fc1_bias_v),
            (vis_slot_h, vis_slot),
        ))
    ]
    for k in (0, 7, 8, 1, 4, 5, 3, 6, 2, 9, 10, 11, 12):
        local[k].start()

    me = place.v
    for k in (0, 7, 8):
        local[k].wait()
    merge_gain = merge_gain_v[...].reshape(1, DV)
    merge_bias = merge_bias_v[...].reshape(1, DV)
    h, r = normalize(xo[...].astype(F32))
    h_out[...] = h
    r_out[...] = r
    value = h * merge_gain + merge_bias
    for t in range(9):
        strips[t] = value[:, 128 * t : 128 * t + 128]
    for p in range(4):
        for t in range(9):
            strip = strips[t, pl.ds(p, SLOTS, stride=4), :]
            rows_in[me, :, pl.ds(DV * p + 128 * t, 128)] = strip.astype(BF16)

    pl.semaphore_wait(barrier, len(near))

    z_copies = []
    for d in (1, 2, 3):
        rows = pl.ds(pl.multiple_of(lax.rem(s + d, 4) * 32, 32), 32)
        z_copies.append(copies.make(grad.at[rows], zin.at[d - 1], place.up(2 * d)))
    for copy in (z_copies[0], z_copies[2], z_copies[1]):
        copy.start()
    gather_in = PlaneGather(place, copies, rows_in, DM, HALF)
    gather_in.start()
    halo_in = [
        copies.make(vit_in, xin.at[1], place.along(1)),
        copies.make(vit_in, xin.at[2], place.along(-1)),
    ]
    gather_grad = PlaneGather(place, copies, rows_grad, DL, DL // 2)
    weights = WeightGather(place, copies, qkv, proj)
    for k in (4, 5):
        local[k].wait()
    weights.start()

    gather_in.near()
    gather_in.pass_on(0)
    gather_in.far()
    gather_in.pass_on(-1)
    gather_in.pass_on(1)
    weights.step(0)
    gather_in.pass_on(2)
    local[1].wait()
    for copy in z_copies:
        copy.wait_recv()

    level = [section_layer[lax.rem(s + 4 - d, 4)] for d in range(4)]
    level = [
        jnp.where(n == 0, 1 / 3, jnp.where(n == 1, 2 / 3, jnp.where(n == 2, 1.0, 0.0))).astype(F32)
        for n in level
    ]

    @pl.loop(0, 4)
    def _(i):
        cols = pl.ds(pl.multiple_of(i * 1024, 128), 1024)
        total = level[0] * zown[:, cols].astype(F32)
        for d in (1, 2, 3):
            total += level[d] * zin[d - 1, :, cols].astype(F32)
        rows_grad[me, :, cols] = total.astype(BF16)

    gather_grad.start()
    for copy in halo_in:
        copy.start()
    weights.step(1)
    gather_in.finish()
    for k in (3, 11):
        local[k].wait()
    fc1_bias = fc1_bias_v[...].reshape(1, HIDDEN)

    def fill_slope(lo, hi):
        @pl.loop(lo, hi)
        def _(i):
            block = rows_in[pl.ds(i * 4, 4)].reshape(128, DM)
            rows = pl.ds(pl.multiple_of(i * 128, 128), 128)
            slope[rows, :] = gelu_slope(dot(block, fc1[...], NT) + fc1_bias)

    gather_grad.near()
    fill_slope(0, 2)
    weights.step(2)
    gather_grad.pass_on(0)
    gather_grad.far()
    fill_slope(2, 4)
    gather_grad.pass_on(-1)
    gather_grad.pass_on(1)
    gather_grad.pass_on(2)
    weights.step(3)
    for k in (2, 6, 9, 10, 12):
        local[k].wait()

    def fill_hidden(offsets):
        blocks = [lax.rem(y + dy + 4, 4) * 4 + lax.rem(x + dx + 4, 4) for dx, dy in offsets]
        rows = jnp.concatenate([rows_grad[i] for i in blocks], axis=0)
        product = dot(rows, fc2[...], NT)
        for k, i in enumerate(blocks):
            hidden[pl.ds(pl.multiple_of(i * 32, 32), 32), :] = product[32 * k : 32 * k + 32]

    for dy in (0, -1, 1):
        fill_hidden([(dx, dy) for dx in (0, -1, 1)])
    gather_grad.finish()
    fill_hidden([(dx, 2) for dx in (0, -1, 1, 2)])
    fill_hidden([(2, dy) for dy in (0, -1, 1)])

    ends = []
    for k in range(16):
        count = image_rows[s, k]
        ends.append(count if k == 0 else ends[-1] + count)
    total_slots = ends[-1]

    shifted = [pltpu.roll(vis_slot[...], lax.rem(32 * q + 128 - 32 * s, 128), 1) for q in range(4)]
    quarter = lax.broadcasted_iota(jnp.int32, (1, 128), 1) // 32
    positions = []
    for t in range(4):
        position = shifted[0][4 * t : 4 * t + 1, :]
        for q in (1, 2, 3):
            position = jnp.where(quarter == q, shifted[q][4 * t + q : 4 * t + q + 1, :], position)
        positions.append(position - 512 * s)
    value = hidden[...]
    high = value.astype(BF16)
    low = (value - high.astype(F32)).astype(BF16)
    for i in range(4):
        slots = lax.broadcasted_iota(jnp.int32, (128, 128), 0) + 128 * i
        placed = jnp.zeros((128, HIDDEN), F32)
        for t in range(4):
            chosen = jnp.where(slots == positions[t], 1.0, 0.0).astype(BF16)
            from_rows = slice(128 * t, 128 * t + 128)
            placed += dot(chosen, high[from_rows]) + dot(chosen, low[from_rows])
        live = lax.broadcasted_iota(jnp.int32, (128, HIDDEN), 0) + 128 * i < total_slots
        block = jnp.where(live, placed, 0.0) * slope[pl.ds(128 * i, 128), :]
        pre_grad[pl.ds(4 * i, 4)] = block.astype(BF16).reshape(4, SLOTS, HIDDEN)

    def token(part, d1, d2):
        dx, dy = (d1, d2) if part == 0 else (d2, d1)
        return lax.rem(y + dy, 4) * 4 + lax.rem(x + dx, 4)

    def first(part, d):
        return place.at(d, 0) if part == 0 else place.at(0, d)

    def second(part, d):
        return place.at(0, d) if part == 0 else place.at(d, 0)

    def product(part, d1):
        block = jnp.concatenate([pre_grad[token(part, d1, d2)] for d2 in range(4)], axis=0)

        @pl.loop(0, 6)
        def _(i):
            start = pl.multiple_of(i * 384, 128)
            cols = pl.ds(pl.multiple_of(start + part * HALF, 128), 384)
            term = dot(block, fc1[:, cols]).astype(BF16).reshape(4, SLOTS, 384)
            ps[part, d1, :, :, pl.ds(start, 384)] = term

    def scatter(part):
        low, high = pl.ds(0, 2), pl.ds(2, 2)
        near1, near2 = first(part, 1), first(part, -1)
        return {
            "1p": copies.make(ps.at[part, 2, low], rb1.at[part, 0], near1),
            "1m": copies.make(ps.at[part, 2, high], rb1.at[part, 1], near2),
            "2p": [copies.make(ps.at[part, 1, k], rb2.at[part, 0, k], near1) for k in range(4)],
            "2m": [copies.make(ps.at[part, 3, k], rb2.at[part, 1, k], near2) for k in range(4)],
            "3": [copies.make(qs.at[part, k - 1], rb3.at[part, k - 1], second(part, k)) for k in (1, 2, 3)],
        }

    sums = [scatter(0), scatter(1)]
    for part in (0, 1):
        product(part, 2)
        sums[part]["1p"].start()
        sums[part]["1m"].start()
    for part in (0, 1):
        product(part, 1)
        for k in (2, 3):
            sums[part]["2p"][k].start()
        product(part, 3)
        for k in (0, 1):
            sums[part]["2m"][k].start()

    weights.step(4)
    def add(part, d1, k, got):
        ps[part, d1, k] = (ps[part, d1, k].astype(F32) + got[...].astype(F32)).astype(BF16)

    for part in (0, 1):
        sums[part]["1p"].wait_recv()
        for k in (1, 0):
            add(part, 1, k, rb1.at[part, 0, k])
            sums[part]["2p"][k].start()
        sums[part]["1m"].wait_recv()
        for k in (3, 2):
            add(part, 3, k, rb1.at[part, 1, k - 2])
            sums[part]["2m"][k].start()
    for part in (0, 1):
        product(part, 0)
    weights.step(5)

    for copy in halo_in:
        copy.wait_recv()
    ln_gain = ln_gain_v[...].reshape(1, DV)
    ln_bias = ln_bias_v[...].reshape(1, DV)

    for w in range(3):
        h, r = normalize(xin[w].astype(F32))
        if w == 0:
            h_in[...] = h
            r_in[...] = r
        xin[w] = (h * ln_gain + ln_bias).astype(BF16)

    def attend(j):
        for i in range(3):
            block = dot(xin[...].reshape(WINDOW, DV), qkv[:, pl.ds(j * DV + i * 384, 384)])
            t32[pl.ds(i * 384, 384), :] = block.T

        @pl.loop(0, HEADS, unroll=2)
        def _(n):
            cols = t32[pl.ds(pl.multiple_of(n * HD, 8), HD), :]
            heads[j * HEADS + n] = cols.astype(BF16)
            if j == 1:
                k_rows[n] = cols.T.astype(BF16)
            if j == 2:
                v_rows[n] = cols.T.astype(BF16)

    weights.finish((0, 1, 2))
    attend(0)
    for k in (2, 3, 1, 0):
        for part in (0, 1):
            sums[part]["2p"][k].wait_recv()
            sums[part]["2m"][k].wait_recv()
            total = (
                ps[part, 0, k].astype(F32)
                + rb2[part, 0, k].astype(F32)
                + rb2[part, 1, k].astype(F32)
            )
            if k:
                qs[part, k - 1] = total.astype(BF16)
                sums[part]["3"][k - 1].start()
            else:
                merge_total[:, pl.ds(part * HALF, HALF)] = total
    attend(1)
    attend(2)

    def image_of(axis):
        shape = (1, WINDOW) if axis else (WINDOW, 1)
        index = lax.broadcasted_iota(jnp.int32, shape, axis)
        back = jnp.where(index < PATCHES, 0, jnp.where(index < 2 * PATCHES, 2 * PATCHES, PATCHES))
        patch = index - back + place.v * PATCHES
        slot = patch >> 2
        image = jnp.zeros(shape, jnp.int32)
        for end in ends:
            image += jnp.where(slot >= end, 1, 0)
        live = (patch >= 0) & (slot < total_slots)
        return jnp.where(live, image, axis - 2), live

    id_row, live_row = image_of(1)
    id_col, _ = image_of(0)
    dead_row = jnp.where(live_row, 0.0, 1.0)

    @pl.loop(0, HEADS, unroll=2)
    def _(n):
        scores = dot(k_rows[n], heads[n]) * SCALE
        allowed = id_col == id_row
        exponent = jnp.where(allowed, jnp.exp(jnp.where(allowed, scores, 0.0)), 0.0)
        denominator = jnp.sum(exponent, axis=0, keepdims=True) + dead_row
        weight = (exponent / denominator).astype(BF16)
        probs[n] = weight
        o_cols[n] = dot(heads[2 * HEADS + n], weight)

    for part in (0, 1):
        cols = pl.ds(part * HALF, HALF)
        for k in (2, 3, 1):
            sums[part]["3"][k - 1].wait_recv()
            merge_total[:, cols] += rb3[part, k - 1].astype(F32)
    for p in range(4):
        for t in range(9):
            strips[t, pl.ds(p, SLOTS, stride=4), :] = merge_total[:, pl.ds(DV * p + 128 * t, 128)]
    for t in range(9):
        wide[:, pl.ds(128 * t, 128)] = strips[t]
    og[0] = normalize_back(wide[...], h_out[...], r_out[...], merge_gain).astype(BF16)
    halo_out = [
        copies.make(og.at[0], og.at[1], place.along(1)),
        copies.make(og.at[0], og.at[2], place.along(-1)),
    ]
    for copy in halo_out:
        copy.start()

    def project_back(w):
        for i in range(3):
            t32[pl.ds(i * 384, 384), pl.ds(w * PATCHES, PATCHES)] = dot(
                proj[pl.ds(i * 384, 384), :], og[w], NT
            )

    weights.step(6)
    weights.finish((3,))
    project_back(0)

    own, others = pl.ds(0, PATCHES), pl.ds(PATCHES, 2 * PATCHES)

    def places(n):
        start = pl.multiple_of(n * HD, 8)
        return [pl.ds(pl.multiple_of(start + j * DV, 8), HD) for j in range(3)]

    @pl.loop(0, HEADS, unroll=4)
    def _(n):
        query, key, value = places(n)
        upstream = t32[query, own].astype(BF16)
        delta = jnp.sum(upstream.astype(F32) * o_cols[n, :, own], axis=0, keepdims=True)
        weight = probs[n, :, own]
        prob = dot(v_rows[n], upstream)
        score = (weight.astype(F32) * (prob - delta) * SCALE).astype(BF16)
        pg[query, :] = dot(heads[HEADS + n], score)
        pg[key, :] = dot(heads[n, :, own], score[:PATCHES], NT)
        pg[value, :] = dot(upstream, weight[:PATCHES], NT)

    for w, copy in ((1, halo_out[0]), (2, halo_out[1])):
        copy.wait_recv()
        project_back(w)

    @pl.loop(0, HEADS, unroll=4)
    def _(n):
        query, key, value = places(n)
        upstream = t32[query, others].astype(BF16)
        delta = jnp.sum(upstream.astype(F32) * o_cols[n, :, others], axis=0, keepdims=True)
        weight = probs[n, own, others]
        prob = dot(v_rows[n, own, :], upstream)
        score = (weight.astype(F32) * (prob - delta) * SCALE).astype(BF16)
        pg[key, :] += dot(heads[n, :, others], score, NT)
        pg[value, :] += dot(upstream, weight, NT)

    projected_grad = pg[...].astype(BF16)
    for i in range(3):
        block = dot(qkv[pl.ds(i * 384, 384), :], projected_grad)
        wide[:, pl.ds(i * 384, 384)] = block.T
    out_ref[...] = (
        og[0].astype(F32) + normalize_back(wide[...], h_in[...], r_in[...], ln_gain)
    ).astype(BF16)
    copies.drain()
    weights.drain()


N_COPIES = 3 + 40 + 2 + 40 + 32 + 26 + 2


def local(
    grad_llm,
    vis_slot,
    image_rows,
    section_layer,
    vit_in,
    vit_out,
    ln_gain,
    ln_bias,
    qkv_weight,
    proj_weight,
    merge_gain,
    merge_bias,
    fc1_weight,
    fc1_bias,
    fc2_weight,
):
    anywhere = pl.BlockSpec(memory_space=pl.ANY)
    vmem = pl.BlockSpec(memory_space=pltpu.VMEM)
    smem = pl.BlockSpec(memory_space=pltpu.SMEM)

    def scratch(shape, dtype=BF16):
        return pltpu.VMEM(shape, dtype)

    return pl.pallas_call(
        body,
        out_shape=jax.ShapeDtypeStruct((PATCHES, DV), BF16),
        in_specs=[anywhere] * 13 + [smem] * 2,
        out_specs=vmem,
        scratch_shapes=[
            scratch((PATCHES, DV)),
            scratch((3, PATCHES, DV)),
            scratch((16, SLOTS, DM)),
            scratch((16, SLOTS, DL)),
            scratch((3, 32, DL)),
            scratch((32, DL)),
            scratch((HIDDEN, DM)),
            scratch((HIDDEN, DL)),
            scratch((DV, 3 * DV)),
            scratch((DV, DV)),
            scratch((PATCHES, DV), F32),
            scratch((PATCHES, 1), F32),
            scratch((PATCHES, DV), F32),
            scratch((PATCHES, 1), F32),
            scratch((PATCHES, DV), F32),
            scratch((512, HIDDEN), F32),
            scratch((512, HIDDEN), F32),
            scratch((16, SLOTS, HIDDEN)),
            scratch((2, 4, 4, SLOTS, HALF)),
            scratch((2, 2, 2, SLOTS, HALF)),
            scratch((2, 2, 4, SLOTS, HALF)),
            scratch((2, 3, SLOTS, HALF)),
            scratch((2, 3, SLOTS, HALF)),
            scratch((SLOTS, DM), F32),
            scratch((3, PATCHES, DV)),
            scratch((DV, WINDOW), F32),
            scratch((3 * HEADS, HD, WINDOW)),
            scratch((HEADS, WINDOW, HD)),
            scratch((HEADS, WINDOW, HD)),
            scratch((HEADS, WINDOW, WINDOW)),
            scratch((HEADS, HD, WINDOW), F32),
            scratch((3 * DV, PATCHES), F32),
            scratch((9, PATCHES, 128), F32),
            scratch((DV,), F32),
            scratch((DV,), F32),
            scratch((DV,), F32),
            scratch((DV,), F32),
            scratch((HIDDEN,), F32),
            scratch((16, 128), jnp.int32),
            pltpu.SemaphoreType.DMA((N_COPIES,)),
            pltpu.SemaphoreType.DMA((N_COPIES,)),
            pltpu.SemaphoreType.DMA((13,)),
        ],
        compiler_params=pltpu.CompilerParams(
            collective_id=0, has_side_effects=True, vmem_limit_bytes=60 * 2**20
        ),
        name="merger_and_attention",
    )(
        grad_llm.reshape(grad_llm.shape[1:]),
        vit_in,
        vit_out,
        qkv_weight,
        proj_weight,
        fc1_weight.T,
        fc2_weight,
        ln_gain,
        ln_bias,
        merge_gain,
        merge_bias,
        fc1_bias,
        vis_slot,
        image_rows,
        section_layer,
    )


def solution(mesh):
    placed = (
        P("section", ("dp", "vit"), None),
        P("dp", None),
        P("dp", None),
        P(),
        P(("dp", "section", "vit"), None),
        P(("dp", "section", "vit"), None),
        P(),
        P(),
        P("section", None),
        P("section", None),
        P(),
        P(),
        P(None, "vit"),
        P("vit"),
        P("vit", None),
    )
    return jax.shard_map(
        local,
        mesh=mesh,
        in_specs=placed,
        out_specs=P(("dp", "section", "vit"), None),
        check_vma=False,
    )
```

```python
import functools

import jax
import jax.numpy as jnp
from jax import lax
from jax.experimental import pallas as pl
from jax.experimental.pallas import tpu as pltpu
from jax.sharding import PartitionSpec as P

HEADS = 16
LEVELS = 3
DV = 1152
DM = 4608
DL = 4096
HD = 72
SLOTS = 32
PATCHES = 128
WINDOW = 384
HIDDEN = 288
HALF = DM // 2
SCALE = HD**-0.5
norm_eps = 1e-06
MESH = pl.DeviceIdType.MESH
F32 = jnp.float32
BF16 = jnp.bfloat16

NN = (((1,), (0,)), ((), ()))
NT = (((1,), (1,)), ((), ()))


def dot(a, b, dims=NN):
    return lax.dot_general(a, b, dims, preferred_element_type=F32)


def normalize(values):
    row_mean = jnp.mean(values, axis=-1, keepdims=True)
    centered = values - row_mean
    variance = jnp.mean(centered * centered, axis=-1, keepdims=True)
    inverse = lax.rsqrt(variance + norm_eps)
    return (centered * inverse, inverse)


def normalize_back(upstream, normed_rows, inverse, gain):
    scaled = upstream * gain
    mean_scaled = jnp.mean(scaled, axis=-1, keepdims=True)
    mean_cross = jnp.mean(scaled * normed_rows, axis=-1, keepdims=True)
    return (scaled - mean_scaled - normed_rows * mean_cross) * inverse


def gelu_slope(pre_act):
    cumulative = 0.5 * (1.0 + lax.erf(pre_act * 0.7071067811865476))
    density = jnp.exp(-0.5 * pre_act * pre_act) * 0.3989422804014327
    return cumulative + pre_act * density


class Place:
    def __init__(self):
        self.s = lax.axis_index("section")
        v = lax.axis_index("vit")
        d = lax.axis_index("dp")
        self.x, self.y = lax.rem(v, 4), v // 4
        self.c, self.zl = lax.rem(d, 2), d // 2
        self.z = self.s * 2 + self.zl
        self.v = v

    def at(self, dx=0, dy=0):
        x, y = lax.rem(self.x + dx + 4, 4), lax.rem(self.y + dy + 4, 4)
        return {"section": self.s, "vit": y * 4 + x, "dp": self.zl * 2 + self.c}

    def up(self, dz):
        z = lax.rem(self.z + dz + 8, 8)
        return {"section": z // 2, "vit": self.v, "dp": lax.rem(z, 2) * 2 + self.c}

    def other_core(self):
        return {"section": self.s, "vit": self.v, "dp": self.zl * 2 + 1 - self.c}

    def along(self, dv):
        return {"section": self.s, "vit": lax.rem(self.v + dv + 16, 16), "dp": self.zl * 2 + self.c}


class Copies:
    def __init__(self, ssem, rsem):
        self.ssem, self.rsem, self.made, self.count = ssem, rsem, [], 0

    def make(self, src, dst, device, drained=True):
        k = self.count
        self.count += 1
        copy = pltpu.make_async_remote_copy(
            src, dst, self.ssem.at[k], self.rsem.at[k], device_id=device, device_id_type=MESH
        )
        if drained:
            self.made.append(copy)
        return copy

    def drain(self):
        for copy in self.made:
            copy.wait_send()


class PlaneGather:
    def __init__(self, place, copies, buf, width, split):
        self.parts = []
        for axis in (0, 1):
            cols = pl.ds(0, split) if axis == 0 else pl.ds(split, width - split)

            def block(d1, d2, axis=axis):
                dx, dy = (d1, d2) if axis == 0 else (d2, d1)
                return lax.rem(place.y + dy + 4, 4) * 4 + lax.rem(place.x + dx + 4, 4)

            def first(d, axis=axis):
                return place.at(d, 0) if axis == 0 else place.at(0, d)

            def second(d, axis=axis):
                return place.at(0, d) if axis == 0 else place.at(d, 0)

            def send(d1, d2, rows, device, block=block, cols=cols):
                ref = buf.at[block(d1, d2), rows, cols]
                return copies.make(ref, ref, device)

            every, low, high = pl.ds(0, 32), pl.ds(0, 16), pl.ds(16, 16)
            part = {
                "s1p": send(0, 0, every, first(1)),
                "s1m": send(0, 0, every, first(-1)),
                "f1p": send(-1, 0, low, first(1)),
                "f1m": send(1, 0, high, first(-1)),
            }
            for d1 in (0, -1, 1, 2):
                part["s2p", d1] = send(d1, 0, every, second(1))
                part["s2m", d1] = send(d1, 0, every, second(-1))
                part["f2p", d1] = send(d1, -1, low, second(1))
                part["f2m", d1] = send(d1, 1, high, second(-1))
            self.parts.append(part)

    def start(self):
        for p in self.parts:
            for k in ("s1p", "s1m", ("s2p", 0), ("s2m", 0)):
                p[k].start()

    def near(self):
        for p in self.parts:
            p["s1p"].wait_recv()
            p["f1p"].start()
            p["s2p", -1].start()
            p["s2m", -1].start()
            p["s1m"].wait_recv()
            p["f1m"].start()
            p["s2p", 1].start()
            p["s2m", 1].start()

    def far(self):
        for p in self.parts:
            p["f1p"].wait_recv()
            p["f1m"].wait_recv()
            p["s2p", 2].start()
            p["s2m", 2].start()

    def pass_on(self, d1):
        for p in self.parts:
            p["s2p", d1].wait_recv()
            p["f2p", d1].start()
            p["s2m", d1].wait_recv()
            p["f2m", d1].start()

    def finish(self):
        for d1 in (0, -1, 1, 2):
            for p in self.parts:
                p["f2p", d1].wait_recv()
                p["f2m", d1].wait_recv()


class WeightGather:
    def __init__(self, place, copies, qkv, proj):
        s, c, zl = place.s, place.c, place.zl
        self.odd = zl == 1
        self.even = zl == 0
        chunks = [
            (qkv, 48, n * 48, 3456, 1792) for n in range(3)
        ] + [(proj, 144, 0, 1152, 640)]

        def piece(chunk, section, side):
            ref, rows, offset, width, split = chunk
            start = pl.multiple_of(lax.rem(section + 8, 4) * 288 + c * 144 + offset, 16)
            cols = {
                0: pl.ds(0, width), 1: pl.ds(0, split), 2: pl.ds(split, width - split)
            }[side]
            return ref.at[pl.ds(start, rows), cols]

        def make(chunk, section, side, device, drained=True):
            ref = piece(chunk, section, side)
            return copies.make(ref, ref, device, drained)

        right, left, core = place.up(1), place.up(-1), place.other_core()
        self.right, self.left = [], []
        for ch in chunks:
            self.right.append((
                make(ch, s - 1 + zl, 0, right, False),
                make(ch, s - 1, 0, core),
                make(ch, s - 2 + zl, 1, right),
                make(ch, s - 2, 1, core),
            ))
            self.left.append((
                make(ch, s + zl, 0, left, False),
                make(ch, s + 1, 0, core),
                make(ch, s + zl + 1, 2, left),
                make(ch, s + 2, 2, core),
            ))

    def each(self):
        return ((self.odd, self.even, self.right), (self.even, self.odd, self.left))

    def start(self):
        for lead, _, side in self.each():
            pl.when(lead)(side[0][0].start)

    def follow_whole(self, n):
        for lead, follow, side in self.each():
            whole, core, _, _ = side[n]
            if n < 3:

                @pl.when(lead)
                def _():
                    whole.wait_send()
                    side[n + 1][0].start()

            @pl.when(follow)
            def _():
                whole.wait_recv()
                core.start()
                whole.start()

    def lead_whole(self, n):
        for lead, _, side in self.each():
            whole, core, part, _ = side[n]

            @pl.when(lead)
            def _():
                whole.wait_recv()
                core.start()
                part.start()

    def follow_part(self, n):
        for _, follow, side in self.each():
            _, _, part, core = side[n]

            @pl.when(follow)
            def _():
                part.wait_recv()
                core.start()
                part.start()

    def lead_part(self, n):
        for lead, _, side in self.each():
            _, _, part, core = side[n]

            @pl.when(lead)
            def _():
                part.wait_recv()
                core.start()

    def step(self, k):
        for n, act in (
            (k, self.follow_whole), (k - 1, self.lead_whole), (k - 2, self.follow_part), (k - 3, self.lead_part)
        ):
            if 0 <= n < 4:
                act(n)

    def finish(self, pieces):
        for side in (self.right, self.left):
            for n in pieces:
                side[n][1].wait_recv()
                side[n][3].wait_recv()

    def drain(self):
        for _, follow, side in self.each():
            for n in range(3):
                pl.when(follow)(side[n][0].wait_send)
            side[3][0].wait_send()


def body(
    grad, vit_in, vit_out, qkv_w, proj_w, fc1_w, fc2_w,
    ln_gain_h, ln_bias_h, merge_gain_h, merge_bias_h, fc1_bias_h, vis_slot_h,
    image_rows, section_layer,
    out_ref,
    xo, xin, rows_in, rows_grad, zin, zown, fc1, fc2, qkv, proj,
    h_out, r_out, h_in, r_in, wide, slope, hidden, pre_grad,
    ps, rb1, rb2, qs, rb3, merge_total, og,
    t32, heads, k_rows, v_rows, probs, o_cols, pg, strips,
    ln_gain_v, ln_bias_v, merge_gain_v, merge_bias_v, fc1_bias_v, vis_slot, ssem, rsem, lsem,
):
    place = Place()
    s, x, y = place.s, place.x, place.y
    copies = Copies(ssem, rsem)

    near = [place.at(1, 0), place.at(-1, 0), place.at(2, 0), place.at(0, 1), place.at(0, -1), place.at(0, 2)]
    near += [place.up(1), place.up(-1), place.up(2), place.up(-2), place.up(4), place.other_core()]
    near += [place.along(1), place.along(-1)]
    barrier = pltpu.get_barrier_semaphore()
    for device in near:
        pl.semaphore_signal(barrier, inc=1, device_id=device, device_id_type=MESH)

    own_rows = pl.ds(pl.multiple_of(s * 288, 16), 288)
    group_rows = pl.ds(pl.multiple_of(s * 32, 32), 32)
    local = [
        pltpu.make_async_copy(src, dst, lsem.at[k])
        for k, (src, dst) in enumerate((
            (vit_out, xo),
            (grad.at[group_rows], zown),
            (vit_in, xin.at[0]),
            (fc1_w, fc1),
            (qkv_w, qkv.at[own_rows]),
            (proj_w, proj.at[own_rows]),
            (fc2_w, fc2),
            (merge_gain_h, merge_gain_v),
            (merge_bias_h, merge_bias_v),
            (ln_gain_h, ln_gain_v),
            (ln_bias_h, ln_bias_v),
            (fc1_bias_h, fc1_bias_v),
            (vis_slot_h, vis_slot),
        ))
    ]
    for k in (0, 7, 8, 1, 4, 5, 3, 6, 2, 9, 10, 11, 12):
        local[k].start()

    me = place.v
    for k in (0, 7, 8):
        local[k].wait()
    merge_gain = merge_gain_v[...].reshape(1, DV)
    merge_bias = merge_bias_v[...].reshape(1, DV)
    h, r = normalize(xo[...].astype(F32))
    h_out[...] = h
    r_out[...] = r
    value = h * merge_gain + merge_bias
    for t in range(9):
        strips[t] = value[:, 128 * t : 128 * t + 128]
    for p in range(4):
        for t in range(9):
            strip = strips[t, pl.ds(p, SLOTS, stride=4), :]
            rows_in[me, :, pl.ds(DV * p + 128 * t, 128)] = strip.astype(BF16)

    pl.semaphore_wait(barrier, len(near))

    z_copies = []
    for d in (1, 2, 3):
        rows = pl.ds(pl.multiple_of(lax.rem(s + d, 4) * 32, 32), 32)
        z_copies.append(copies.make(grad.at[rows], zin.at[d - 1], place.up(2 * d)))
    for copy in (z_copies[0], z_copies[2], z_copies[1]):
        copy.start()
    gather_in = PlaneGather(place, copies, rows_in, DM, HALF)
    gather_in.start()
    halo_in = [
        copies.make(vit_in, xin.at[1], place.along(1)),
        copies.make(vit_in, xin.at[2], place.along(-1)),
    ]
    gather_grad = PlaneGather(place, copies, rows_grad, DL, DL // 2)
    weights = WeightGather(place, copies, qkv, proj)
    for k in (4, 5):
        local[k].wait()
    weights.start()

    gather_in.near()
    gather_in.pass_on(0)
    gather_in.far()
    gather_in.pass_on(-1)
    gather_in.pass_on(1)
    weights.step(0)
    gather_in.pass_on(2)
    local[1].wait()
    for copy in z_copies:
        copy.wait_recv()

    level = [section_layer[lax.rem(s + 4 - d, 4)] for d in range(4)]
    level = [
        jnp.where(n == 0, 1 / 3, jnp.where(n == 1, 2 / 3, jnp.where(n == 2, 1.0, 0.0))).astype(F32)
        for n in level
    ]

    @pl.loop(0, 4)
    def _(i):
        cols = pl.ds(pl.multiple_of(i * 1024, 128), 1024)
        total = level[0] * zown[:, cols].astype(F32)
        for d in (1, 2, 3):
            total += level[d] * zin[d - 1, :, cols].astype(F32)
        rows_grad[me, :, cols] = total.astype(BF16)

    gather_grad.start()
    for copy in halo_in:
        copy.start()
    weights.step(1)
    gather_in.finish()
    for k in (3, 11):
        local[k].wait()
    fc1_bias = fc1_bias_v[...].reshape(1, HIDDEN)

    def fill_slope(lo, hi):
        @pl.loop(lo, hi)
        def _(i):
            block = rows_in[pl.ds(i * 4, 4)].reshape(128, DM)
            rows = pl.ds(pl.multiple_of(i * 128, 128), 128)
            slope[rows, :] = gelu_slope(dot(block, fc1[...], NT) + fc1_bias)

    gather_grad.near()
    fill_slope(0, 2)
    weights.step(2)
    gather_grad.pass_on(0)
    gather_grad.far()
    fill_slope(2, 4)
    gather_grad.pass_on(-1)
    gather_grad.pass_on(1)
    for k in (2, 9, 10):
        local[k].wait()
    for copy in halo_in:
        copy.wait_recv()
    ln_gain = ln_gain_v[...].reshape(1, DV)
    ln_bias = ln_bias_v[...].reshape(1, DV)

    for w in range(3):
        h, r = normalize(xin[w].astype(F32))
        if w == 0:
            h_in[...] = h
            r_in[...] = r
        xin[w] = (h * ln_gain + ln_bias).astype(BF16)

    gather_grad.pass_on(2)
    weights.step(3)
    for k in (6, 12):
        local[k].wait()

    def fill_hidden(offsets):
        blocks = [lax.rem(y + dy + 4, 4) * 4 + lax.rem(x + dx + 4, 4) for dx, dy in offsets]
        rows = jnp.concatenate([rows_grad[i] for i in blocks], axis=0)
        product = dot(rows, fc2[...], NT)
        for k, i in enumerate(blocks):
            hidden[pl.ds(pl.multiple_of(i * 32, 32), 32), :] = product[32 * k : 32 * k + 32]

    for dy in (0, -1, 1):
        fill_hidden([(dx, dy) for dx in (0, -1, 1)])
    gather_grad.finish()
    fill_hidden([(dx, 2) for dx in (0, -1, 1, 2)])
    fill_hidden([(2, dy) for dy in (0, -1, 1)])

    ends = []
    for k in range(16):
        count = image_rows[s, k]
        ends.append(count if k == 0 else ends[-1] + count)
    total_slots = ends[-1]

    shifted = [pltpu.roll(vis_slot[...], lax.rem(32 * q + 128 - 32 * s, 128), 1) for q in range(4)]
    quarter = lax.broadcasted_iota(jnp.int32, (1, 128), 1) // 32
    positions = []
    for t in range(4):
        position = shifted[0][4 * t : 4 * t + 1, :]
        for q in (1, 2, 3):
            position = jnp.where(quarter == q, shifted[q][4 * t + q : 4 * t + q + 1, :], position)
        positions.append(position - 512 * s)
    value = hidden[...]
    high = value.astype(BF16)
    low = (value - high.astype(F32)).astype(BF16)
    for i in range(4):
        slots = lax.broadcasted_iota(jnp.int32, (128, 128), 0) + 128 * i
        placed = jnp.zeros((128, HIDDEN), F32)
        for t in range(4):
            chosen = jnp.where(slots == positions[t], 1.0, 0.0).astype(BF16)
            from_rows = slice(128 * t, 128 * t + 128)
            placed += dot(chosen, high[from_rows]) + dot(chosen, low[from_rows])
        live = lax.broadcasted_iota(jnp.int32, (128, HIDDEN), 0) + 128 * i < total_slots
        block = jnp.where(live, placed, 0.0) * slope[pl.ds(128 * i, 128), :]
        pre_grad[pl.ds(4 * i, 4)] = block.astype(BF16).reshape(4, SLOTS, HIDDEN)

    def token(part, d1, d2):
        dx, dy = (d1, d2) if part == 0 else (d2, d1)
        return lax.rem(y + dy, 4) * 4 + lax.rem(x + dx, 4)

    def first(part, d):
        return place.at(d, 0) if part == 0 else place.at(0, d)

    def second(part, d):
        return place.at(0, d) if part == 0 else place.at(d, 0)

    def product(part, d1):
        block = jnp.concatenate([pre_grad[token(part, d1, d2)] for d2 in range(4)], axis=0)

        @pl.loop(0, 6)
        def _(i):
            start = pl.multiple_of(i * 384, 128)
            cols = pl.ds(pl.multiple_of(start + part * HALF, 128), 384)
            term = dot(block, fc1[:, cols]).astype(BF16).reshape(4, SLOTS, 384)
            ps[part, d1, :, :, pl.ds(start, 384)] = term

    def scatter(part):
        low, high = pl.ds(0, 2), pl.ds(2, 2)
        near1, near2 = first(part, 1), first(part, -1)
        return {
            "1p": copies.make(ps.at[part, 2, low], rb1.at[part, 0], near1),
            "1m": copies.make(ps.at[part, 2, high], rb1.at[part, 1], near2),
            "2p": [copies.make(ps.at[part, 1, k], rb2.at[part, 0, k], near1) for k in range(4)],
            "2m": [copies.make(ps.at[part, 3, k], rb2.at[part, 1, k], near2) for k in range(4)],
            "3": [copies.make(qs.at[part, k - 1], rb3.at[part, k - 1], second(part, k)) for k in (1, 2, 3)],
        }

    sums = [scatter(0), scatter(1)]
    for part in (0, 1):
        product(part, 2)
        sums[part]["1p"].start()
        sums[part]["1m"].start()
    for part in (0, 1):
        product(part, 1)
        for k in (2, 3):
            sums[part]["2p"][k].start()
        product(part, 3)
        for k in (0, 1):
            sums[part]["2m"][k].start()

    weights.step(4)
    def add(part, d1, k, got):
        ps[part, d1, k] = (ps[part, d1, k].astype(F32) + got[...].astype(F32)).astype(BF16)

    for part in (0, 1):
        sums[part]["1p"].wait_recv()
        for k in (1, 0):
            add(part, 1, k, rb1.at[part, 0, k])
            sums[part]["2p"][k].start()
        sums[part]["1m"].wait_recv()
        for k in (3, 2):
            add(part, 3, k, rb1.at[part, 1, k - 2])
            sums[part]["2m"][k].start()
    for part in (0, 1):
        product(part, 0)
    weights.step(5)

    def attend(j):
        for i in range(3):
            block = dot(xin[...].reshape(WINDOW, DV), qkv[:, pl.ds(j * DV + i * 384, 384)])
            t32[pl.ds(i * 384, 384), :] = block.T

        @pl.loop(0, HEADS, unroll=4)
        def _(n):
            cols = t32[pl.ds(pl.multiple_of(n * HD, 8), HD), :]
            heads[j * HEADS + n] = cols.astype(BF16)
            if j == 1:
                k_rows[n] = cols.T.astype(BF16)
            if j == 2:
                v_rows[n] = cols.T.astype(BF16)

    weights.finish((0, 1, 2))
    attend(0)
    attend(1)
    attend(2)
    for k in (2, 3, 1, 0):
        for part in (0, 1):
            sums[part]["2p"][k].wait_recv()
            sums[part]["2m"][k].wait_recv()
            total = (
                ps[part, 0, k].astype(F32)
                + rb2[part, 0, k].astype(F32)
                + rb2[part, 1, k].astype(F32)
            )
            if k:
                qs[part, k - 1] = total.astype(BF16)
                sums[part]["3"][k - 1].start()
            else:
                merge_total[:, pl.ds(part * HALF, HALF)] = total

    def image_of(axis):
        shape = (1, WINDOW) if axis else (WINDOW, 1)
        index = lax.broadcasted_iota(jnp.int32, shape, axis)
        back = jnp.where(index < PATCHES, 0, jnp.where(index < 2 * PATCHES, 2 * PATCHES, PATCHES))
        patch = index - back + place.v * PATCHES
        slot = patch >> 2
        image = jnp.zeros(shape, jnp.int32)
        for end in ends:
            image += jnp.where(slot >= end, 1, 0)
        live = (patch >= 0) & (slot < total_slots)
        return jnp.where(live, image, axis - 2), live

    id_row, live_row = image_of(1)
    id_col, _ = image_of(0)
    dead_row = jnp.where(live_row, 0.0, 1.0)

    @pl.loop(0, HEADS, unroll=4)
    def _(n):
        scores = dot(k_rows[n], heads[n]) * SCALE
        allowed = id_col == id_row
        exponent = jnp.where(allowed, jnp.exp(jnp.where(allowed, scores, 0.0)), 0.0)
        denominator = jnp.sum(exponent, axis=0, keepdims=True) + dead_row
        weight = (exponent / denominator).astype(BF16)
        probs[n] = weight
        o_cols[n] = dot(heads[2 * HEADS + n], weight)

    for part in (0, 1):
        cols = pl.ds(part * HALF, HALF)
        for k in (2, 3, 1):
            sums[part]["3"][k - 1].wait_recv()
            merge_total[:, cols] += rb3[part, k - 1].astype(F32)
    for p in range(4):
        for t in range(9):
            strips[t, pl.ds(p, SLOTS, stride=4), :] = merge_total[:, pl.ds(DV * p + 128 * t, 128)]
    for t in range(9):
        wide[:, pl.ds(128 * t, 128)] = strips[t]
    og[0] = normalize_back(wide[...], h_out[...], r_out[...], merge_gain).astype(BF16)
    halo_out = [
        copies.make(og.at[0], og.at[1], place.along(1)),
        copies.make(og.at[0], og.at[2], place.along(-1)),
    ]
    for copy in halo_out:
        copy.start()

    def project_back(w):
        for i in range(3):
            t32[pl.ds(i * 384, 384), pl.ds(w * PATCHES, PATCHES)] = dot(
                proj[pl.ds(i * 384, 384), :], og[w], NT
            )

    weights.step(6)
    weights.finish((3,))
    project_back(0)

    own, others = pl.ds(0, PATCHES), pl.ds(PATCHES, 2 * PATCHES)

    def places(n):
        start = pl.multiple_of(n * HD, 8)
        return [pl.ds(pl.multiple_of(start + j * DV, 8), HD) for j in range(3)]

    @pl.loop(0, HEADS, unroll=4)
    def _(n):
        query, key, value = places(n)
        upstream = t32[query, own].astype(BF16)
        delta = jnp.sum(upstream.astype(F32) * o_cols[n, :, own], axis=0, keepdims=True)
        weight = probs[n, :, own]
        prob = dot(v_rows[n], upstream)
        score = (weight.astype(F32) * (prob - delta) * SCALE).astype(BF16)
        pg[query, :] = dot(heads[HEADS + n], score)
        pg[key, :] = dot(heads[n, :, own], score[:PATCHES], NT)
        pg[value, :] = dot(upstream, weight[:PATCHES], NT)

    for w, copy in ((1, halo_out[0]), (2, halo_out[1])):
        copy.wait_recv()
        project_back(w)

    @pl.loop(0, HEADS, unroll=4)
    def _(n):
        query, key, value = places(n)
        upstream = t32[query, others].astype(BF16)
        delta = jnp.sum(upstream.astype(F32) * o_cols[n, :, others], axis=0, keepdims=True)
        weight = probs[n, own, others]
        prob = dot(v_rows[n, own, :], upstream)
        score = (weight.astype(F32) * (prob - delta) * SCALE).astype(BF16)
        pg[key, :] += dot(heads[n, :, others], score, NT)
        pg[value, :] += dot(upstream, weight, NT)

    projected_grad = pg[...].astype(BF16)
    for i in range(3):
        block = dot(qkv[pl.ds(i * 384, 384), :], projected_grad)
        wide[:, pl.ds(i * 384, 384)] = block.T
    out_ref[...] = (
        og[0].astype(F32) + normalize_back(wide[...], h_in[...], r_in[...], ln_gain)
    ).astype(BF16)
    copies.drain()
    weights.drain()


N_COPIES = 3 + 40 + 2 + 40 + 32 + 26 + 2


def local(
    grad_llm,
    vis_slot,
    image_rows,
    section_layer,
    vit_in,
    vit_out,
    ln_gain,
    ln_bias,
    qkv_weight,
    proj_weight,
    merge_gain,
    merge_bias,
    fc1_weight,
    fc1_bias,
    fc2_weight,
):
    anywhere = pl.BlockSpec(memory_space=pl.ANY)
    vmem = pl.BlockSpec(memory_space=pltpu.VMEM)
    smem = pl.BlockSpec(memory_space=pltpu.SMEM)

    def scratch(shape, dtype=BF16):
        return pltpu.VMEM(shape, dtype)

    return pl.pallas_call(
        body,
        out_shape=jax.ShapeDtypeStruct((PATCHES, DV), BF16),
        in_specs=[anywhere] * 13 + [smem] * 2,
        out_specs=vmem,
        scratch_shapes=[
            scratch((PATCHES, DV)),
            scratch((3, PATCHES, DV)),
            scratch((16, SLOTS, DM)),
            scratch((16, SLOTS, DL)),
            scratch((3, 32, DL)),
            scratch((32, DL)),
            scratch((HIDDEN, DM)),
            scratch((HIDDEN, DL)),
            scratch((DV, 3 * DV)),
            scratch((DV, DV)),
            scratch((PATCHES, DV), F32),
            scratch((PATCHES, 1), F32),
            scratch((PATCHES, DV), F32),
            scratch((PATCHES, 1), F32),
            scratch((PATCHES, DV), F32),
            scratch((512, HIDDEN), F32),
            scratch((512, HIDDEN), F32),
            scratch((16, SLOTS, HIDDEN)),
            scratch((2, 4, 4, SLOTS, HALF)),
            scratch((2, 2, 2, SLOTS, HALF)),
            scratch((2, 2, 4, SLOTS, HALF)),
            scratch((2, 3, SLOTS, HALF)),
            scratch((2, 3, SLOTS, HALF)),
            scratch((SLOTS, DM), F32),
            scratch((3, PATCHES, DV)),
            scratch((DV, WINDOW), F32),
            scratch((3 * HEADS, HD, WINDOW)),
            scratch((HEADS, WINDOW, HD)),
            scratch((HEADS, WINDOW, HD)),
            scratch((HEADS, WINDOW, WINDOW)),
            scratch((HEADS, HD, WINDOW), F32),
            scratch((3 * DV, PATCHES), F32),
            scratch((9, PATCHES, 128), F32),
            scratch((DV,), F32),
            scratch((DV,), F32),
            scratch((DV,), F32),
            scratch((DV,), F32),
            scratch((HIDDEN,), F32),
            scratch((16, 128), jnp.int32),
            pltpu.SemaphoreType.DMA((N_COPIES,)),
            pltpu.SemaphoreType.DMA((N_COPIES,)),
            pltpu.SemaphoreType.DMA((13,)),
        ],
        compiler_params=pltpu.CompilerParams(
            collective_id=0, has_side_effects=True, vmem_limit_bytes=60 * 2**20
        ),
        name="merger_and_attention",
    )(
        grad_llm.reshape(grad_llm.shape[1:]),
        vit_in,
        vit_out,
        qkv_weight,
        proj_weight,
        fc1_weight.T,
        fc2_weight,
        ln_gain,
        ln_bias,
        merge_gain,
        merge_bias,
        fc1_bias,
        vis_slot,
        image_rows,
        section_layer,
    )


def solution(mesh):
    placed = (
        P("section", ("dp", "vit"), None),
        P("dp", None),
        P("dp", None),
        P(),
        P(("dp", "section", "vit"), None),
        P(("dp", "section", "vit"), None),
        P(),
        P(),
        P("section", None),
        P("section", None),
        P(),
        P(),
        P(None, "vit"),
        P("vit"),
        P("vit", None),
    )
    return jax.shard_map(
        local,
        mesh=mesh,
        in_specs=placed,
        out_specs=P(("dp", "section", "vit"), None),
        check_vma=False,
    )
```

```python
import functools

import jax
import jax.numpy as jnp
from jax import lax
from jax.experimental import pallas as pl
from jax.experimental.pallas import tpu as pltpu
from jax.sharding import PartitionSpec as P

HEADS = 16
LEVELS = 3
DV = 1152
DM = 4608
DL = 4096
HD = 72
SLOTS = 32
PATCHES = 128
WINDOW = 384
HIDDEN = 288
HALF = DM // 2
SCALE = HD**-0.5
norm_eps = 1e-06
MESH = pl.DeviceIdType.MESH
F32 = jnp.float32
BF16 = jnp.bfloat16

NN = (((1,), (0,)), ((), ()))
NT = (((1,), (1,)), ((), ()))


def dot(a, b, dims=NN):
    return lax.dot_general(a, b, dims, preferred_element_type=F32)


def normalize(values):
    row_mean = jnp.mean(values, axis=-1, keepdims=True)
    centered = values - row_mean
    variance = jnp.mean(centered * centered, axis=-1, keepdims=True)
    inverse = lax.rsqrt(variance + norm_eps)
    return (centered * inverse, inverse)


def normalize_back(upstream, normed_rows, inverse, gain):
    scaled = upstream * gain
    mean_scaled = jnp.mean(scaled, axis=-1, keepdims=True)
    mean_cross = jnp.mean(scaled * normed_rows, axis=-1, keepdims=True)
    return (scaled - mean_scaled - normed_rows * mean_cross) * inverse


def gelu_slope(pre_act):
    cumulative = 0.5 * (1.0 + lax.erf(pre_act * 0.7071067811865476))
    density = jnp.exp(-0.5 * pre_act * pre_act) * 0.3989422804014327
    return cumulative + pre_act * density


class Place:
    def __init__(self):
        self.s = lax.axis_index("section")
        v = lax.axis_index("vit")
        d = lax.axis_index("dp")
        self.x, self.y = lax.rem(v, 4), v // 4
        self.c, self.zl = lax.rem(d, 2), d // 2
        self.z = self.s * 2 + self.zl
        self.v = v

    def at(self, dx=0, dy=0):
        x, y = lax.rem(self.x + dx + 4, 4), lax.rem(self.y + dy + 4, 4)
        return {"section": self.s, "vit": y * 4 + x, "dp": self.zl * 2 + self.c}

    def up(self, dz):
        z = lax.rem(self.z + dz + 8, 8)
        return {"section": z // 2, "vit": self.v, "dp": lax.rem(z, 2) * 2 + self.c}

    def other_core(self):
        return {"section": self.s, "vit": self.v, "dp": self.zl * 2 + 1 - self.c}

    def along(self, dv):
        return {"section": self.s, "vit": lax.rem(self.v + dv + 16, 16), "dp": self.zl * 2 + self.c}


class Copies:
    def __init__(self, ssem, rsem):
        self.ssem, self.rsem, self.made, self.count = ssem, rsem, [], 0

    def make(self, src, dst, device, drained=True):
        k = self.count
        self.count += 1
        copy = pltpu.make_async_remote_copy(
            src, dst, self.ssem.at[k], self.rsem.at[k], device_id=device, device_id_type=MESH
        )
        if drained:
            self.made.append(copy)
        return copy

    def drain(self):
        for copy in self.made:
            copy.wait_send()


class PlaneGather:
    def __init__(self, place, copies, buf, width, split):
        self.parts = []
        for axis in (0, 1):
            cols = pl.ds(0, split) if axis == 0 else pl.ds(split, width - split)

            def block(d1, d2, axis=axis):
                dx, dy = (d1, d2) if axis == 0 else (d2, d1)
                return lax.rem(place.y + dy + 4, 4) * 4 + lax.rem(place.x + dx + 4, 4)

            def first(d, axis=axis):
                return place.at(d, 0) if axis == 0 else place.at(0, d)

            def second(d, axis=axis):
                return place.at(0, d) if axis == 0 else place.at(d, 0)

            def send(d1, d2, rows, device, block=block, cols=cols):
                ref = buf.at[block(d1, d2), rows, cols]
                return copies.make(ref, ref, device)

            every, low, high = pl.ds(0, 32), pl.ds(0, 16), pl.ds(16, 16)
            part = {
                "s1p": send(0, 0, every, first(1)),
                "s1m": send(0, 0, every, first(-1)),
                "f1p": send(-1, 0, low, first(1)),
                "f1m": send(1, 0, high, first(-1)),
            }
            for d1 in (0, -1, 1, 2):
                part["s2p", d1] = send(d1, 0, every, second(1))
                part["s2m", d1] = send(d1, 0, every, second(-1))
                part["f2p", d1] = send(d1, -1, low, second(1))
                part["f2m", d1] = send(d1, 1, high, second(-1))
            self.parts.append(part)

    def start(self):
        for p in self.parts:
            for k in ("s1p", "s1m", ("s2p", 0), ("s2m", 0)):
                p[k].start()

    def near(self):
        for p in self.parts:
            p["s1p"].wait_recv()
            p["f1p"].start()
            p["s2p", -1].start()
            p["s2m", -1].start()
            p["s1m"].wait_recv()
            p["f1m"].start()
            p["s2p", 1].start()
            p["s2m", 1].start()

    def far(self):
        for p in self.parts:
            p["f1p"].wait_recv()
            p["f1m"].wait_recv()
            p["s2p", 2].start()
            p["s2m", 2].start()

    def pass_on(self, d1):
        for p in self.parts:
            p["s2p", d1].wait_recv()
            p["f2p", d1].start()
            p["s2m", d1].wait_recv()
            p["f2m", d1].start()

    def finish(self):
        for d1 in (0, -1, 1, 2):
            for p in self.parts:
                p["f2p", d1].wait_recv()
                p["f2m", d1].wait_recv()


class WeightGather:
    def __init__(self, place, copies, qkv, proj):
        s, c, zl = place.s, place.c, place.zl
        self.odd = zl == 1
        self.even = zl == 0
        chunks = [
            (qkv, 48, n * 48, 3456, 1792) for n in range(3)
        ] + [(proj, 144, 0, 1152, 640)]

        def piece(chunk, section, side):
            ref, rows, offset, width, split = chunk
            start = pl.multiple_of(lax.rem(section + 8, 4) * 288 + c * 144 + offset, 16)
            cols = {
                0: pl.ds(0, width), 1: pl.ds(0, split), 2: pl.ds(split, width - split)
            }[side]
            return ref.at[pl.ds(start, rows), cols]

        def make(chunk, section, side, device, drained=True):
            ref = piece(chunk, section, side)
            return copies.make(ref, ref, device, drained)

        right, left, core = place.up(1), place.up(-1), place.other_core()
        self.right, self.left = [], []
        for ch in chunks:
            self.right.append((
                make(ch, s - 1 + zl, 0, right, False),
                make(ch, s - 1, 0, core),
                make(ch, s - 2 + zl, 1, right),
                make(ch, s - 2, 1, core),
            ))
            self.left.append((
                make(ch, s + zl, 0, left, False),
                make(ch, s + 1, 0, core),
                make(ch, s + zl + 1, 2, left),
                make(ch, s + 2, 2, core),
            ))

    def each(self):
        return ((self.odd, self.even, self.right), (self.even, self.odd, self.left))

    def start(self):
        for lead, _, side in self.each():
            pl.when(lead)(side[0][0].start)

    def follow_whole(self, n):
        for lead, follow, side in self.each():
            whole, core, _, _ = side[n]
            if n < 3:

                @pl.when(lead)
                def _():
                    whole.wait_send()
                    side[n + 1][0].start()

            @pl.when(follow)
            def _():
                whole.wait_recv()
                core.start()
                whole.start()

    def lead_whole(self, n):
        for lead, _, side in self.each():
            whole, core, part, _ = side[n]

            @pl.when(lead)
            def _():
                whole.wait_recv()
                core.start()
                part.start()

    def follow_part(self, n):
        for _, follow, side in self.each():
            _, _, part, core = side[n]

            @pl.when(follow)
            def _():
                part.wait_recv()
                core.start()
                part.start()

    def lead_part(self, n):
        for lead, _, side in self.each():
            _, _, part, core = side[n]

            @pl.when(lead)
            def _():
                part.wait_recv()
                core.start()

    def step(self, k):
        for n, act in (
            (k, self.follow_whole), (k - 1, self.lead_whole), (k - 2, self.follow_part), (k - 3, self.lead_part)
        ):
            if 0 <= n < 4:
                act(n)

    def finish(self, pieces):
        for side in (self.right, self.left):
            for n in pieces:
                side[n][1].wait_recv()
                side[n][3].wait_recv()

    def drain(self):
        for _, follow, side in self.each():
            for n in range(3):
                pl.when(follow)(side[n][0].wait_send)
            side[3][0].wait_send()


def body(
    grad, vit_in, vit_out, qkv_w, proj_w, fc1_w, fc2_w,
    ln_gain_h, ln_bias_h, merge_gain_h, merge_bias_h, fc1_bias_h, vis_slot_h,
    image_rows, section_layer,
    out_ref,
    xo, xin, rows_in, rows_grad, zin, zown, fc1, fc2, qkv, proj,
    h_out, r_out, h_in, r_in, wide, slope, hidden, pre_grad,
    ps, rb1, rb2, qs, rb3, merge_total, og,
    t32, heads, k_rows, v_rows, probs, o_cols, pg, strips,
    ln_gain_v, ln_bias_v, merge_gain_v, merge_bias_v, fc1_bias_v, vis_slot, ssem, rsem, lsem,
):
    place = Place()
    s, x, y = place.s, place.x, place.y
    copies = Copies(ssem, rsem)

    near = [place.at(1, 0), place.at(-1, 0), place.at(2, 0), place.at(0, 1), place.at(0, -1), place.at(0, 2)]
    near += [place.up(1), place.up(-1), place.up(2), place.up(-2), place.up(4), place.other_core()]
    near += [place.along(1), place.along(-1)]
    barrier = pltpu.get_barrier_semaphore()
    for device in near:
        pl.semaphore_signal(barrier, inc=1, device_id=device, device_id_type=MESH)

    own_rows = pl.ds(pl.multiple_of(s * 288, 16), 288)
    group_rows = pl.ds(pl.multiple_of(s * 32, 32), 32)
    local = [
        pltpu.make_async_copy(src, dst, lsem.at[k])
        for k, (src, dst) in enumerate((
            (vit_out, xo),
            (grad.at[group_rows], zown),
            (vit_in, xin.at[0]),
            (fc1_w, fc1),
            (qkv_w, qkv.at[own_rows]),
            (proj_w, proj.at[own_rows]),
            (fc2_w, fc2),
            (merge_gain_h, merge_gain_v),
            (merge_bias_h, merge_bias_v),
            (ln_gain_h, ln_gain_v),
            (ln_bias_h, ln_bias_v),
            (fc1_bias_h, fc1_bias_v),
            (vis_slot_h, vis_slot),
        ))
    ]
    for k in (0, 7, 8, 1, 4, 5, 3, 6, 2, 9, 10, 11, 12):
        local[k].start()

    me = place.v
    for k in (0, 7, 8):
        local[k].wait()
    merge_gain = merge_gain_v[...].reshape(1, DV)
    merge_bias = merge_bias_v[...].reshape(1, DV)
    h, r = normalize(xo[...].astype(F32))
    h_out[...] = h
    r_out[...] = r
    value = h * merge_gain + merge_bias
    for t in range(9):
        strips[t] = value[:, 128 * t : 128 * t + 128]
    for p in range(4):
        for t in range(9):
            strip = strips[t, pl.ds(p, SLOTS, stride=4), :]
            rows_in[me, :, pl.ds(DV * p + 128 * t, 128)] = strip.astype(BF16)

    pl.semaphore_wait(barrier, len(near))

    z_copies = []
    for d in (1, 2, 3):
        rows = pl.ds(pl.multiple_of(lax.rem(s + d, 4) * 32, 32), 32)
        z_copies.append(copies.make(grad.at[rows], zin.at[d - 1], place.up(2 * d)))
    for copy in (z_copies[0], z_copies[2], z_copies[1]):
        copy.start()
    gather_in = PlaneGather(place, copies, rows_in, DM, HALF)
    gather_in.start()
    halo_in = [
        copies.make(vit_in, xin.at[1], place.along(1)),
        copies.make(vit_in, xin.at[2], place.along(-1)),
    ]
    gather_grad = PlaneGather(place, copies, rows_grad, DL, DL // 2)
    weights = WeightGather(place, copies, qkv, proj)
    for k in (4, 5):
        local[k].wait()
    weights.start()

    gather_in.near()
    gather_in.pass_on(0)
    gather_in.far()
    gather_in.pass_on(-1)
    gather_in.pass_on(1)
    weights.step(0)
    gather_in.pass_on(2)
    local[1].wait()
    for copy in z_copies:
        copy.wait_recv()

    level = [section_layer[lax.rem(s + 4 - d, 4)] for d in range(4)]
    level = [
        jnp.where(n == 0, 1 / 3, jnp.where(n == 1, 2 / 3, jnp.where(n == 2, 1.0, 0.0))).astype(F32)
        for n in level
    ]

    @pl.loop(0, 4)
    def _(i):
        cols = pl.ds(pl.multiple_of(i * 1024, 128), 1024)
        total = level[0] * zown[:, cols].astype(F32)
        for d in (1, 2, 3):
            total += level[d] * zin[d - 1, :, cols].astype(F32)
        rows_grad[me, :, cols] = total.astype(BF16)

    gather_grad.start()
    for copy in halo_in:
        copy.start()
    weights.step(1)
    gather_in.finish()
    for k in (3, 11):
        local[k].wait()
    fc1_bias = fc1_bias_v[...].reshape(1, HIDDEN)

    def fill_slope(lo, hi):
        @pl.loop(lo, hi)
        def _(i):
            block = rows_in[pl.ds(i * 4, 4)].reshape(128, DM)
            rows = pl.ds(pl.multiple_of(i * 128, 128), 128)
            slope[rows, :] = gelu_slope(dot(block, fc1[...], NT) + fc1_bias)

    gather_grad.near()
    fill_slope(0, 2)
    weights.step(2)
    gather_grad.pass_on(0)
    gather_grad.far()
    fill_slope(2, 4)
    gather_grad.pass_on(-1)
    gather_grad.pass_on(1)
    for k in (2, 9, 10):
        local[k].wait()
    for copy in halo_in:
        copy.wait_recv()
    ln_gain = ln_gain_v[...].reshape(1, DV)
    ln_bias = ln_bias_v[...].reshape(1, DV)

    for w in range(3):
        h, r = normalize(xin[w].astype(F32))
        if w == 0:
            h_in[...] = h
            r_in[...] = r
        xin[w] = (h * ln_gain + ln_bias).astype(BF16)

    gather_grad.pass_on(2)
    weights.step(3)
    for k in (6, 12):
        local[k].wait()

    def fill_hidden(offsets):
        blocks = [lax.rem(y + dy + 4, 4) * 4 + lax.rem(x + dx + 4, 4) for dx, dy in offsets]
        rows = jnp.concatenate([rows_grad[i] for i in blocks], axis=0)
        product = dot(rows, fc2[...], NT)
        for k, i in enumerate(blocks):
            hidden[pl.ds(pl.multiple_of(i * 32, 32), 32), :] = product[32 * k : 32 * k + 32]

    for dy in (0, -1, 1):
        fill_hidden([(dx, dy) for dx in (0, -1, 1)])
    gather_grad.finish()
    fill_hidden([(dx, 2) for dx in (0, -1, 1, 2)])
    fill_hidden([(2, dy) for dy in (0, -1, 1)])

    ends = []
    for k in range(16):
        count = image_rows[s, k]
        ends.append(count if k == 0 else ends[-1] + count)
    total_slots = ends[-1]

    shifted = [pltpu.roll(vis_slot[...], lax.rem(32 * q + 128 - 32 * s, 128), 1) for q in range(4)]
    quarter = lax.broadcasted_iota(jnp.int32, (1, 128), 1) // 32
    positions = []
    for t in range(4):
        position = shifted[0][4 * t : 4 * t + 1, :]
        for q in (1, 2, 3):
            position = jnp.where(quarter == q, shifted[q][4 * t + q : 4 * t + q + 1, :], position)
        positions.append(position - 512 * s)
    value = hidden[...]
    high = value.astype(BF16)
    low = (value - high.astype(F32)).astype(BF16)
    for i in range(4):
        slots = lax.broadcasted_iota(jnp.int32, (128, 128), 0) + 128 * i
        placed = jnp.zeros((128, HIDDEN), F32)
        for t in range(4):
            chosen = jnp.where(slots == positions[t], 1.0, 0.0).astype(BF16)
            from_rows = slice(128 * t, 128 * t + 128)
            placed += dot(chosen, high[from_rows]) + dot(chosen, low[from_rows])
        live = lax.broadcasted_iota(jnp.int32, (128, HIDDEN), 0) + 128 * i < total_slots
        block = jnp.where(live, placed, 0.0) * slope[pl.ds(128 * i, 128), :]
        pre_grad[pl.ds(4 * i, 4)] = block.astype(BF16).reshape(4, SLOTS, HIDDEN)

    def token(part, d1, d2):
        dx, dy = (d1, d2) if part == 0 else (d2, d1)
        return lax.rem(y + dy, 4) * 4 + lax.rem(x + dx, 4)

    def first(part, d):
        return place.at(d, 0) if part == 0 else place.at(0, d)

    def second(part, d):
        return place.at(0, d) if part == 0 else place.at(d, 0)

    def product(part, d1):
        block = jnp.concatenate([pre_grad[token(part, d1, d2)] for d2 in range(4)], axis=0)

        @pl.loop(0, 6)
        def _(i):
            start = pl.multiple_of(i * 384, 128)
            cols = pl.ds(pl.multiple_of(start + part * HALF, 128), 384)
            term = dot(block, fc1[:, cols]).astype(BF16).reshape(4, SLOTS, 384)
            ps[part, d1, :, :, pl.ds(start, 384)] = term

    def scatter(part):
        low, high = pl.ds(0, 2), pl.ds(2, 2)
        near1, near2 = first(part, 1), first(part, -1)
        return {
            "1p": copies.make(ps.at[part, 2, low], rb1.at[part, 0], near1),
            "1m": copies.make(ps.at[part, 2, high], rb1.at[part, 1], near2),
            "2p": [copies.make(ps.at[part, 1, k], rb2.at[part, 0, k], near1) for k in range(4)],
            "2m": [copies.make(ps.at[part, 3, k], rb2.at[part, 1, k], near2) for k in range(4)],
            "3": [copies.make(qs.at[part, k - 1], rb3.at[part, k - 1], second(part, k)) for k in (1, 2, 3)],
        }

    sums = [scatter(0), scatter(1)]
    for part in (0, 1):
        product(part, 2)
        sums[part]["1p"].start()
        sums[part]["1m"].start()
    for part in (0, 1):
        product(part, 1)
        for k in (2, 3):
            sums[part]["2p"][k].start()
        product(part, 3)
        for k in (0, 1):
            sums[part]["2m"][k].start()

    weights.step(4)
    def add(part, d1, k, got):
        ps[part, d1, k] = (ps[part, d1, k].astype(F32) + got[...].astype(F32)).astype(BF16)

    for part in (0, 1):
        sums[part]["1p"].wait_recv()
        for k in (1, 0):
            add(part, 1, k, rb1.at[part, 0, k])
            sums[part]["2p"][k].start()
        sums[part]["1m"].wait_recv()
        for k in (3, 2):
            add(part, 3, k, rb1.at[part, 1, k - 2])
            sums[part]["2m"][k].start()
    for part in (0, 1):
        product(part, 0)
    weights.step(5)

    def attend(j):
        for i in range(3):
            block = dot(xin[...].reshape(WINDOW, DV), qkv[:, pl.ds(j * DV + i * 384, 384)])
            t32[pl.ds(i * 384, 384), :] = block.T

        @pl.loop(0, HEADS, unroll=4)
        def _(n):
            cols = t32[pl.ds(pl.multiple_of(n * HD, 8), HD), :]
            heads[j * HEADS + n] = cols.astype(BF16)
            if j == 1:
                k_rows[n] = cols.T.astype(BF16)
            if j == 2:
                v_rows[n] = cols.T.astype(BF16)

    weights.finish((0, 1, 2))
    attend(0)
    attend(1)
    attend(2)
    for k in (2, 3, 1, 0):
        for part in (0, 1):
            sums[part]["2p"][k].wait_recv()
            sums[part]["2m"][k].wait_recv()
            total = (
                ps[part, 0, k].astype(F32)
                + rb2[part, 0, k].astype(F32)
                + rb2[part, 1, k].astype(F32)
            )
            if k:
                qs[part, k - 1] = total.astype(BF16)
                sums[part]["3"][k - 1].start()
            else:
                merge_total[:, pl.ds(part * HALF, HALF)] = total

    def image_of(axis):
        shape = (1, WINDOW) if axis else (WINDOW, 1)
        index = lax.broadcasted_iota(jnp.int32, shape, axis)
        back = jnp.where(index < PATCHES, 0, jnp.where(index < 2 * PATCHES, 2 * PATCHES, PATCHES))
        patch = index - back + place.v * PATCHES
        slot = patch >> 2
        image = jnp.zeros(shape, jnp.int32)
        for end in ends:
            image += jnp.where(slot >= end, 1, 0)
        live = (patch >= 0) & (slot < total_slots)
        return jnp.where(live, image, axis - 2), live

    id_row, live_row = image_of(1)
    id_col, _ = image_of(0)
    dead_row = jnp.where(live_row, 0.0, 1.0)

    @pl.loop(0, HEADS, unroll=4)
    def _(n):
        scores = dot(k_rows[n], heads[n]) * SCALE
        allowed = id_col == id_row
        exponent = jnp.where(allowed, jnp.exp(jnp.where(allowed, scores, 0.0)), 0.0)
        denominator = jnp.sum(exponent, axis=0, keepdims=True) + dead_row
        weight = (exponent / denominator).astype(BF16)
        probs[n] = weight
        o_cols[n] = dot(heads[2 * HEADS + n], weight)

    for part in (0, 1):
        cols = pl.ds(part * HALF, HALF)
        for k in (2, 3, 1):
            sums[part]["3"][k - 1].wait_recv()
            merge_total[:, cols] += rb3[part, k - 1].astype(F32)
    for p in range(4):
        for t in range(9):
            strips[t, pl.ds(p, SLOTS, stride=4), :] = merge_total[:, pl.ds(DV * p + 128 * t, 128)]
    for t in range(9):
        wide[:, pl.ds(128 * t, 128)] = strips[t]
    og[0] = normalize_back(wide[...], h_out[...], r_out[...], merge_gain).astype(BF16)
    halo_out = [
        copies.make(og.at[0], og.at[1], place.along(1)),
        copies.make(og.at[0], og.at[2], place.along(-1)),
    ]
    for copy in halo_out:
        copy.start()

    def project_back(w):
        for i in range(3):
            t32[pl.ds(i * 384, 384), pl.ds(w * PATCHES, PATCHES)] = dot(
                proj[pl.ds(i * 384, 384), :], og[w], NT
            )

    weights.step(6)
    weights.finish((3,))
    project_back(0)

    own, others = pl.ds(0, PATCHES), pl.ds(PATCHES, 2 * PATCHES)

    def places(n):
        start = pl.multiple_of(n * HD, 8)
        return [pl.ds(pl.multiple_of(start + j * DV, 8), HD) for j in range(3)]

    @pl.loop(0, HEADS, unroll=4)
    def _(n):
        query, key, value = places(n)
        upstream = t32[query, own].astype(BF16)
        delta = jnp.sum(upstream.astype(F32) * o_cols[n, :, own], axis=0, keepdims=True)
        weight = probs[n, :, own]
        prob = dot(v_rows[n], upstream)
        score = (weight.astype(F32) * (prob - delta) * SCALE).astype(BF16)
        pg[query, :] = dot(heads[HEADS + n], score)
        pg[key, :] = dot(heads[n, :, own], score[:PATCHES], NT)
        pg[value, :] = dot(upstream, weight[:PATCHES], NT)

    query_grad = pg[pl.ds(0, DV), :].astype(BF16)
    for i in range(3):
        rows = pl.ds(i * 384, 384)
        t32[rows, own] = dot(qkv[rows, pl.ds(0, DV)], query_grad)

    for w, copy in ((1, halo_out[0]), (2, halo_out[1])):
        copy.wait_recv()
        project_back(w)

    @pl.loop(0, HEADS, unroll=4)
    def _(n):
        query, key, value = places(n)
        upstream = t32[query, others].astype(BF16)
        delta = jnp.sum(upstream.astype(F32) * o_cols[n, :, others], axis=0, keepdims=True)
        weight = probs[n, own, others]
        prob = dot(v_rows[n, own, :], upstream)
        score = (weight.astype(F32) * (prob - delta) * SCALE).astype(BF16)
        pg[key, :] += dot(heads[n, :, others], score, NT)
        pg[value, :] += dot(upstream, weight, NT)

    key_value_grad = pg[pl.ds(DV, 2 * DV), :].astype(BF16)
    for i in range(3):
        rows = pl.ds(i * 384, 384)
        block = t32[rows, own] + dot(qkv[rows, pl.ds(DV, 2 * DV)], key_value_grad)
        wide[:, rows] = block.T
    out_ref[...] = (
        og[0].astype(F32) + normalize_back(wide[...], h_in[...], r_in[...], ln_gain)
    ).astype(BF16)
    copies.drain()
    weights.drain()


N_COPIES = 3 + 40 + 2 + 40 + 32 + 26 + 2


def local(
    grad_llm,
    vis_slot,
    image_rows,
    section_layer,
    vit_in,
    vit_out,
    ln_gain,
    ln_bias,
    qkv_weight,
    proj_weight,
    merge_gain,
    merge_bias,
    fc1_weight,
    fc1_bias,
    fc2_weight,
):
    anywhere = pl.BlockSpec(memory_space=pl.ANY)
    vmem = pl.BlockSpec(memory_space=pltpu.VMEM)
    smem = pl.BlockSpec(memory_space=pltpu.SMEM)

    def scratch(shape, dtype=BF16):
        return pltpu.VMEM(shape, dtype)

    return pl.pallas_call(
        body,
        out_shape=jax.ShapeDtypeStruct((PATCHES, DV), BF16),
        in_specs=[anywhere] * 13 + [smem] * 2,
        out_specs=vmem,
        scratch_shapes=[
            scratch((PATCHES, DV)),
            scratch((3, PATCHES, DV)),
            scratch((16, SLOTS, DM)),
            scratch((16, SLOTS, DL)),
            scratch((3, 32, DL)),
            scratch((32, DL)),
            scratch((HIDDEN, DM)),
            scratch((HIDDEN, DL)),
            scratch((DV, 3 * DV)),
            scratch((DV, DV)),
            scratch((PATCHES, DV), F32),
            scratch((PATCHES, 1), F32),
            scratch((PATCHES, DV), F32),
            scratch((PATCHES, 1), F32),
            scratch((PATCHES, DV), F32),
            scratch((512, HIDDEN), F32),
            scratch((512, HIDDEN), F32),
            scratch((16, SLOTS, HIDDEN)),
            scratch((2, 4, 4, SLOTS, HALF)),
            scratch((2, 2, 2, SLOTS, HALF)),
            scratch((2, 2, 4, SLOTS, HALF)),
            scratch((2, 3, SLOTS, HALF)),
            scratch((2, 3, SLOTS, HALF)),
            scratch((SLOTS, DM), F32),
            scratch((3, PATCHES, DV)),
            scratch((DV, WINDOW), F32),
            scratch((3 * HEADS, HD, WINDOW)),
            scratch((HEADS, WINDOW, HD)),
            scratch((HEADS, WINDOW, HD)),
            scratch((HEADS, WINDOW, WINDOW)),
            scratch((HEADS, HD, WINDOW), F32),
            scratch((3 * DV, PATCHES), F32),
            scratch((9, PATCHES, 128), F32),
            scratch((DV,), F32),
            scratch((DV,), F32),
            scratch((DV,), F32),
            scratch((DV,), F32),
            scratch((HIDDEN,), F32),
            scratch((16, 128), jnp.int32),
            pltpu.SemaphoreType.DMA((N_COPIES,)),
            pltpu.SemaphoreType.DMA((N_COPIES,)),
            pltpu.SemaphoreType.DMA((13,)),
        ],
        compiler_params=pltpu.CompilerParams(
            collective_id=0, has_side_effects=True, vmem_limit_bytes=60 * 2**20
        ),
        name="merger_and_attention",
    )(
        grad_llm.reshape(grad_llm.shape[1:]),
        vit_in,
        vit_out,
        qkv_weight,
        proj_weight,
        fc1_weight.T,
        fc2_weight,
        ln_gain,
        ln_bias,
        merge_gain,
        merge_bias,
        fc1_bias,
        vis_slot,
        image_rows,
        section_layer,
    )


def solution(mesh):
    placed = (
        P("section", ("dp", "vit"), None),
        P("dp", None),
        P("dp", None),
        P(),
        P(("dp", "section", "vit"), None),
        P(("dp", "section", "vit"), None),
        P(),
        P(),
        P("section", None),
        P("section", None),
        P(),
        P(),
        P(None, "vit"),
        P("vit"),
        P("vit", None),
    )
    return jax.shard_map(
        local,
        mesh=mesh,
        in_specs=placed,
        out_specs=P(("dp", "section", "vit"), None),
        check_vma=False,
    )
```
